512 devices in a mesh: seq: 64 (over y, z), head: 8 (over x, core).
Axes of the slice: x: 4, y: 4, z: 16, core: 2. Of those that a mesh axis runs over, the one named last changes fastest.
Arguments:
- ssm_input: bfloat16 [65536, 4096], P('seq', 'head'), may hold values from -125 to 125
- gate_input: bfloat16 [65536, 4096], P('seq', 'head'), may hold values from -8 to 8
- write_proj: bfloat16 [65536, 128], P('seq'), may hold values from -0.1875 to 0.1875
- read_proj: bfloat16 [65536, 128], P('seq'), may hold values from -0.5 to 0.5
- decay_codes: int32 [32, 65536], P('head', 'seq'), may hold values from 1 to 131072
- decay_rate: float32 [32], P('head'), may hold values from 0.8 to 6000
- skip_gain: float32 [32], P('head'), may hold values from 0.5 to 1.5
- norm_gain: float32 [4096], P('head'), may hold values from 0.5 to 1.5
Outputs:
- mamba_out: bfloat16 [65536, 4096], P('seq', 'head')
The draws below stay inside these ranges and needn't reach their ends.
All inputs are finite; a program needn't handle non-finite values.
Results may differ from the reference program's by a relative error of at most 0.0054.
Values sent between devices are 32-bit elements; how exact they have to be, the bound alone decides.
No kernel may reach another device: no remote copies, remote signals or barrier semaphores. Data moves between devices by JAX's collectives and lax.ppermute only.
A program may use at most 64 MiB of HBM per device.

```python
import jax
import jax.numpy as jnp
from jax import lax

HEADS = 32
HEAD_DIM = 128
STATE = 128
GROUP = 256
TOK_DEV = 1024
TOKENS = 65536


def draw_ssm_input(key, part):
    first = jax.random.fold_in(key, 0)
    third = jax.random.fold_in(key, 2)
    width = HEADS * HEAD_DIM
    columns = jnp.arange(width, dtype=jnp.float32) / width
    base = jnp.clip(jax.random.normal(first, (TOKENS, width), jnp.float32), -5.0, 5.0)
    row_scale = 10.0 ** jax.random.uniform(third, (TOKENS, 1), jnp.float32)
    values = base * row_scale * 10.0 ** columns[None, :] / 4.0
    return values.astype(jnp.bfloat16)


def draw_decay_rate(key, part):
    first, second, third = jax.random.split(key, 3)
    slow_rate = 0.8 * 3.0 ** jax.random.uniform(first, (HEADS,), jnp.float32)
    fast_rate = 2.4 * 2500.0 ** jax.random.uniform(second, (HEADS,), jnp.float32)
    chosen = jax.random.bernoulli(third, 0.5, (HEADS,))
    return jnp.where(chosen, fast_rate, slow_rate)


def draw_decay_codes(key, part):
    first, second, third = jax.random.split(key, 3)
    base = jax.random.randint(first, (HEADS, TOKENS // TOK_DEV, TOK_DEV), 1, 4)
    factor = jax.random.randint(second, (HEADS, TOKENS // TOK_DEV, 1), 1, 3)
    codes = (base * factor).reshape(HEADS, TOKENS)
    spots = jax.random.randint(third, (3,), 0, TOKENS)
    places = jnp.arange(TOKENS, dtype=jnp.int32)
    struck = jnp.any(places[None, :] == spots[:, None], axis=0)
    return jnp.where(struck[None, :], 2 * TOKENS, codes).astype(jnp.int32)


def block_levels(stream_key, shape, pieces, smallest, high):
    level, own = 1.0, jax.random.fold_in(stream_key, 6)
    for axis_at, parts in pieces:
        heights = jnp.exp(jax.random.uniform(jax.random.fold_in(own, axis_at), (parts,), jnp.float32, smallest / len(pieces), high / len(pieces)))
        level = level * jnp.repeat(heights, shape[axis_at] // parts).reshape([-1 if axis == axis_at else 1 for axis in range(len(shape))])
    return level


def noise(stream_key, extent, scale, reach, pieces=(), kind=jnp.bfloat16):
    loudness = block_levels(stream_key, extent, pieces, -0.22, 0.18) if pieces else 1.0
    values = jax.random.normal(stream_key, extent, jnp.float32) * scale * loudness
    return jnp.minimum(jnp.maximum(values, -reach), reach).astype(kind)


def setup_inputs(seed: int = 0) -> dict:
    seeds = jax.random.split(jax.random.key(seed), 9)
    ssm_input = draw_ssm_input(jax.random.fold_in(seeds[8], 71), 0)
    gate_input = noise(seeds[1], (TOKENS, HEADS * HEAD_DIM), 1.5, 8.0, ((0, 64), (1, 8)))
    write_proj = noise(seeds[2], (TOKENS, STATE), TOK_DEV ** -0.5, 0.1875, ((0, 64),))
    read_proj = noise(seeds[3], (TOKENS, STATE), STATE ** -0.5, 0.5, ((0, 64),))
    decay_codes = draw_decay_codes(jax.random.fold_in(seeds[8], 71), 0)
    decay_rate = draw_decay_rate(jax.random.fold_in(seeds[8], 71), 0)
    skip_gain = jnp.clip(0.5 + 1.0 * jax.random.uniform(seeds[6], (HEADS,), jnp.float32) ** block_levels(seeds[6], (HEADS,), ((0, 8),), -0.2, 0.2), 0.5, 1.5)
    norm_gain = jnp.clip(1.0 + 0.1 * jax.random.normal(seeds[7], (HEADS * HEAD_DIM,), jnp.float32), 0.5, 1.5)
    return {"ssm_input": ssm_input, "gate_input": gate_input, "write_proj": write_proj, "read_proj": read_proj, "decay_codes": decay_codes, "decay_rate": decay_rate, "skip_gain": skip_gain, "norm_gain": norm_gain}


def reference(ssm_input, gate_input, write_proj, read_proj, decay_codes, decay_rate, skip_gain, norm_gain):
    block_count = TOKENS // GROUP
    log_decay = -(decay_codes.astype(jnp.float32) * decay_rate[:, None]) / (8.0 * TOKENS)
    cumulative = jnp.cumsum(log_decay.reshape(HEADS, block_count, GROUP), axis=2)
    x_blocks = ssm_input.reshape(block_count, GROUP, HEADS, HEAD_DIM)
    write_blocks = write_proj.reshape(block_count, GROUP, STATE)
    read_blocks = read_proj.reshape(block_count, GROUP, STATE)
    positions = jnp.arange(GROUP, dtype=jnp.int32)
    causal = positions[:, None] >= positions[None, :]

    def one_head(head_index):
        head_x = lax.dynamic_index_in_dim(x_blocks, head_index, 2, keepdims=False)
        head_cum = lax.dynamic_index_in_dim(cumulative, head_index, 0, keepdims=False)

        def block_step(running, block_items):
            x_part, write_part, read_part, cum_part = block_items
            scores = jnp.dot(read_part, write_part.T, preferred_element_type=jnp.float32)
            spread = cum_part[:, None] - cum_part[None, :]
            decay_mask = jnp.where(causal, jnp.exp(jnp.where(causal, spread, 0.0)), 0.0)
            mixing = (decay_mask * scores).astype(jnp.bfloat16)
            inner_out = jnp.dot(mixing, x_part, preferred_element_type=jnp.float32)
            carried = jnp.exp(cum_part)[:, None] * jnp.dot(read_part, running.astype(jnp.bfloat16), preferred_element_type=jnp.float32)
            weighted = (jnp.exp(cum_part[-1] - cum_part)[:, None] * x_part.astype(jnp.float32)).astype(jnp.bfloat16)
            block_state = jnp.dot(write_part.T, weighted, preferred_element_type=jnp.float32)
            running = jnp.exp(cum_part[-1]) * running + block_state
            return (running, inner_out + carried)
        start = jnp.zeros((STATE, HEAD_DIM), jnp.float32)
        _, head_out = lax.scan(block_step, start, (head_x, write_blocks, read_blocks, head_cum))
        return head_out
    head_out = lax.map(one_head, jnp.arange(HEADS, dtype=jnp.int32))
    ssm_out = head_out.transpose(1, 2, 0, 3).reshape(TOKENS, HEADS * HEAD_DIM)
    ssm_out = ssm_out + jnp.repeat(skip_gain, HEAD_DIM)[None, :] * ssm_input.astype(jnp.float32)
    gated_out = ssm_out * jax.nn.silu(gate_input.astype(jnp.float32))
    row_power = lax.optimization_barrier(jnp.mean(gated_out * gated_out, axis=1, keepdims=True))
    return (gated_out * lax.rsqrt(row_power + 1e-05) * norm_gain[None, :]).astype(jnp.bfloat16)
```

```python
import functools
import math

import jax
import jax.numpy as jnp
from jax import lax
from jax.experimental import pallas as pl
from jax.experimental.pallas import tpu as pltpu
from jax.sharding import Mesh
from jax.sharding import PartitionSpec as P

GROUP = 256
HALF = 128
LANES = 128
CODE_SCALE = 524288.0
CHANNELS = 4096
EPS = 1e-05
Y, Z, HEAD = 4, 16, 8
PIECE = 32
PIECE_ROWS = 40
MIB = 1 << 20
NT = (((1,), (1,)), ((), ()))
TN = (((0,), (0,)), ((), ()))


def matmul(a, b, dims=(((1,), (0,)), ((), ()))):
    return lax.dot_general(a, b, dims, preferred_element_type=jnp.float32)


def lower_triangle(size):
    row = lax.broadcasted_iota(jnp.int32, (size, size), 0)
    column = lax.broadcasted_iota(jnp.int32, (size, size), 1)
    return row >= column


def code_parts(codes, heads, blocks):
    rows = jnp.concatenate([codes[:, k * GROUP : (k + 1) * GROUP] for k in range(blocks)], axis=0)
    parts = [rows & 255, (rows >> 8) & 255, rows >> 16]
    return jnp.concatenate([part.astype(jnp.float32) for part in parts], axis=0).astype(jnp.bfloat16)


def joined(sums, axis):
    count = sums.shape[axis] // 3
    low, middle, high = (lax.slice_in_dim(sums, i * count, (i + 1) * count, axis=axis) for i in range(3))
    return low + 256.0 * middle + 65536.0 * high


def code_columns(parts, triangle):
    return joined(matmul(triangle, parts, NT), 1)


def code_rows(parts, triangle):
    return joined(matmul(parts, triangle, NT), 0)


def exponent_row(rate_ref, heads, blocks):
    lane = lax.broadcasted_iota(jnp.int32, (1, blocks * heads), 1)
    row = jnp.zeros((1, blocks * heads), jnp.float32)
    for h in range(heads):
        row = jnp.where(lax.rem(lane, heads) == h, rate_ref[h], row)
    return row * (-1.0 / (CODE_SCALE * math.log(2.0)))


def head_lanes(row, start, heads):
    return jnp.concatenate(
        [jnp.broadcast_to(row[:, start + h : start + h + 1], (1, LANES)) for h in range(heads)], axis=1
    )


def summary_kernel(heads, blocks, rate_ref, codes_ref, write_ref, x_ref, piece_ref, local_ref):
    triangle = lower_triangle(GROUP).astype(jnp.float32).astype(jnp.bfloat16)
    sums = code_columns(code_parts(codes_ref[...], heads, blocks), triangle)
    scale = exponent_row(rate_ref, heads, blocks)
    ends = sums[GROUP - 1 : GROUP, :]
    tail = jnp.exp2((ends - sums) * scale)
    block_decay = jnp.exp2(ends * scale)
    state = None
    for k in range(blocks):
        rows = pl.ds(k * GROUP, GROUP)
        weighted = jnp.concatenate(
            [
                (tail[:, k * heads + h : k * heads + h + 1] * x_ref[rows, h * LANES : (h + 1) * LANES].astype(jnp.float32))
                .astype(jnp.bfloat16)
                for h in range(heads)
            ],
            axis=1,
        )
        added = matmul(write_ref[rows, :], weighted, TN)
        if k:
            local_ref[k - 1] = state
            state = head_lanes(block_decay, k * heads, heads) * state + added
        else:
            state = added
    total = sum(ends[:, k * heads : (k + 1) * heads] for k in range(blocks))
    section_decay = jnp.exp2(total * scale[:, :heads])
    quarters = Z // heads
    for h in range(heads):
        decay = jnp.broadcast_to(section_decay[:, h : h + 1], (PIECE_ROWS - PIECE, LANES))
        for q in range(quarters):
            piece_ref[h * quarters + q, :PIECE, :] = state[q * PIECE : (q + 1) * PIECE, h * LANES : (h + 1) * LANES]
            piece_ref[h * quarters + q, PIECE:, :] = decay


def inner_kernel(
    heads, blocks, rate_ref, skip_ref, codes_ref, write_ref, read_ref, x_ref, gate_ref, base_ref, factor_ref, lead_ref
):
    causal = lower_triangle(GROUP)
    triangle = causal.astype(jnp.float32).astype(jnp.bfloat16)
    corner = lower_triangle(HALF)
    parts = code_parts(codes_ref[...], heads, blocks)
    columns = code_columns(parts, triangle)
    across = code_rows(parts, triangle)
    scale = exponent_row(rate_ref, heads, blocks)
    grown = jnp.exp2(columns * scale)
    ends = columns[GROUP - 1 : GROUP, :]
    before = jnp.zeros((1, heads), jnp.float32)
    for k in range(blocks):
        lead_ref[k : k + 1, :] = head_lanes(jnp.exp2(before * scale[:, :heads]), 0, heads)
        before = before + ends[:, k * heads : (k + 1) * heads]
    for k in range(blocks):
        rows = pl.ds(k * GROUP, GROUP)
        scores = matmul(read_ref[rows, :], write_ref[rows, :], NT)
        for h in range(heads):
            at = k * heads + h
            lanes = slice(h * LANES, (h + 1) * LANES)
            factor = scale[:, h : h + 1]
            column = columns[:, at : at + 1]
            row = across[at : at + 1, :]

            def mixed(t0, t1, s0, s1, masked):
                decay = jnp.exp2((column[t0:t1] - row[:, s0:s1]) * factor) * scores[t0:t1, s0:s1]
                if masked:
                    decay = jnp.where(corner, decay, 0.0)
                return decay.astype(jnp.bfloat16)

            x_part = x_ref[rows, lanes]
            upper = matmul(mixed(0, HALF, 0, HALF, True), x_part[:HALF])
            lower = jnp.concatenate(
                [mixed(HALF, GROUP, 0, HALF, False), mixed(HALF, GROUP, HALF, GROUP, True)], axis=1
            )
            inner = jnp.concatenate([upper, matmul(lower, x_part)], axis=0)
            gate = gate_ref[rows, lanes].astype(jnp.float32)
            silu = gate / (1.0 + jnp.exp(-gate))
            base_ref[rows, lanes] = (inner + skip_ref[h] * x_part.astype(jnp.float32)) * silu
            factor_ref[rows, lanes] = grown[:, at : at + 1] * silu


def scan_kernel(got_ref, prefix_ref, decay_ref, total_ref):
    state = jnp.zeros((PIECE, LANES), jnp.float32)
    decay = jnp.ones((PIECE_ROWS - PIECE, LANES), jnp.float32)
    for i in range(Z):
        prefix_ref[i] = state
        decay_ref[i] = decay
        step = got_ref[i, PIECE:, :]
        state = step[:1] * state + got_ref[i, :PIECE, :]
        decay = step * decay
    for j in range(Y):
        total_ref[j, :PIECE, :] = state
        total_ref[j, PIECE:, :] = decay


def join_kernel(totals_ref, prefix_ref, decay_ref, out_ref):
    mine = lax.axis_index("y")
    state = jnp.zeros((PIECE, LANES), jnp.float32)
    for j in range(Y - 1):
        state = jnp.where(j < mine, totals_ref[j, PIECE : PIECE + 1, :] * state + totals_ref[j, :PIECE, :], state)
    for i in range(Z):
        out_ref[i] = decay_ref[i, :1, :] * state + prefix_ref[i]


def carry_kernel(heads, blocks, entering_ref, local_ref, lead_ref, read_ref, base_ref, factor_ref, gated_ref, power_ref):
    quarters = Z // heads
    entering = jnp.concatenate(
        [
            jnp.concatenate([entering_ref[h * quarters + q] for q in range(quarters)], axis=0)
            for h in range(heads)
        ],
        axis=1,
    )
    sums = []
    for k in range(blocks):
        rows = pl.ds(k * GROUP, GROUP)
        state = lead_ref[k : k + 1, :] * entering + local_ref[k - 1] if k else entering
        read_out = matmul(read_ref[rows, :], state.astype(jnp.bfloat16))
        gated = base_ref[rows, :] + factor_ref[rows, :] * read_out
        gated_ref[rows, :] = gated
        squares = gated * gated
        squares = sum(squares[:, h * LANES : (h + 1) * LANES] for h in range(heads))
        for half in range(GROUP // LANES):
            sums.append(jnp.sum(squares[half * LANES : (half + 1) * LANES].T, axis=0, keepdims=True))
    sums = jnp.concatenate(sums, axis=0)
    for j in range(HEAD):
        power_ref[j] = sums


def norm_kernel(heads, power_ref, gain_ref, gated_ref, out_ref):
    power = sum(power_ref[j] for j in range(HEAD)) * (1.0 / CHANNELS)
    scale = lax.rsqrt(power + EPS)
    for r in range(scale.shape[0]):
        rows = pl.ds(r * LANES, LANES)
        column = jnp.broadcast_to(scale[r : r + 1, :], (LANES, LANES)).T
        for h in range(heads):
            lanes = slice(h * LANES, (h + 1) * LANES)
            out_ref[rows, lanes] = (gated_ref[rows, lanes] * column * gain_ref[:, lanes]).astype(jnp.bfloat16)


VMEM = pl.BlockSpec(memory_space=pltpu.VMEM)
SMEM = pl.BlockSpec(memory_space=pltpu.SMEM)


def call(kernel, out_shapes, in_specs, limit, flops, moved):
    return pl.pallas_call(
        kernel,
        out_shape=tuple(jax.ShapeDtypeStruct(shape, dtype) for shape, dtype in out_shapes),
        in_specs=in_specs,
        out_specs=tuple(VMEM for _ in out_shapes),
        compiler_params=pltpu.CompilerParams(vmem_limit_bytes=limit),
        cost_estimate=pl.CostEstimate(flops=flops, bytes_accessed=moved, transcendentals=0),
    )


def local(ssm_input, gate_input, write_proj, read_proj, decay_codes, decay_rate, skip_gain, norm_gain):
    rows, width = ssm_input.shape
    heads = decay_rate.shape[0]
    blocks = rows // GROUP
    f32 = jnp.float32
    piece, own = call(
        functools.partial(summary_kernel, heads, blocks),
        (((Z, PIECE_ROWS, LANES), f32), ((blocks - 1, LANES, width), f32)),
        [SMEM, VMEM, VMEM, VMEM],
        16 * MIB,
        1 << 28,
        3 * MIB,
    )(decay_rate, decay_codes, write_proj, ssm_input)
    got = lax.all_to_all(piece, "z", 0, 0, tiled=True)
    base, factor, lead = call(
        functools.partial(inner_kernel, heads, blocks),
        (((rows, width), f32), ((rows, width), f32), ((blocks, width), f32)),
        [SMEM, SMEM, VMEM, VMEM, VMEM, VMEM, VMEM],
        24 * MIB,
        1 << 30,
        7 * MIB,
    )(decay_rate, skip_gain, decay_codes, write_proj, read_proj, ssm_input, gate_input)
    prefix, prefix_decay, total = call(
        scan_kernel,
        (((Z, PIECE, LANES), f32), ((Z, PIECE_ROWS - PIECE, LANES), f32), ((Y, PIECE_ROWS, LANES), f32)),
        [VMEM],
        8 * MIB,
        1 << 20,
        MIB,
    )(got)
    totals = lax.all_to_all(total, "y", 0, 0, tiled=True)
    (joint,) = call(
        join_kernel, (((Z, PIECE, LANES), f32),), [VMEM, VMEM, VMEM], 8 * MIB, 1 << 20, MIB
    )(totals, prefix, prefix_decay)
    entering = lax.all_to_all(joint, "z", 0, 0, tiled=True)
    gated, power = call(
        functools.partial(carry_kernel, heads, blocks),
        (((rows, width), f32), ((HEAD, rows // LANES, LANES), f32)),
        [VMEM] * 6,
        16 * MIB,
        1 << 28,
        8 * MIB,
    )(entering, own, lead, read_proj, base, factor)
    powers = lax.all_to_all(power, "head", 0, 0, tiled=True)
    (out,) = call(
        functools.partial(norm_kernel, heads), (((rows, width), jnp.bfloat16),), [VMEM] * 3, 8 * MIB, 1 << 20, 3 * MIB
    )(powers, norm_gain.reshape(1, width), gated)
    return out


def solution(mesh):
    split = Mesh(mesh.devices.reshape(Y, Z, HEAD), ("y", "z", "head"))
    seq = ("y", "z")
    placed = (
        P(seq, "head"),
        P(seq, "head"),
        P(seq, None),
        P(seq, None),
        P("head", seq),
        P("head"),
        P("head"),
        P("head"),
    )
    return jax.shard_map(local, mesh=split, in_specs=placed, out_specs=P(seq, "head"), check_vma=False)
```

```python
import functools
import math

import jax
import jax.numpy as jnp
from jax import lax
from jax.experimental import pallas as pl
from jax.experimental.pallas import tpu as pltpu
from jax.sharding import Mesh
from jax.sharding import PartitionSpec as P

GROUP = 256
HALF = 128
LANES = 128
CODE_SCALE = 524288.0
CHANNELS = 4096
EPS = 1e-05
Y, Z, HEAD = 4, 16, 8
PIECE = 32
PIECE_ROWS = 40
MIB = 1 << 20
NT = (((1,), (1,)), ((), ()))
TN = (((0,), (0,)), ((), ()))


def matmul(a, b, dims=(((1,), (0,)), ((), ()))):
    return lax.dot_general(a, b, dims, preferred_element_type=jnp.float32)


def lower_triangle(size):
    row = lax.broadcasted_iota(jnp.int32, (size, size), 0)
    column = lax.broadcasted_iota(jnp.int32, (size, size), 1)
    return row >= column


def code_parts(codes, heads, blocks):
    rows = jnp.concatenate([codes[:, k * GROUP : (k + 1) * GROUP] for k in range(blocks)], axis=0)
    parts = [rows & 255, (rows >> 8) & 255, rows >> 16]
    return jnp.concatenate([part.astype(jnp.float32) for part in parts], axis=0).astype(jnp.bfloat16)


def joined(sums, axis):
    count = sums.shape[axis] // 3
    low, middle, high = (lax.slice_in_dim(sums, i * count, (i + 1) * count, axis=axis) for i in range(3))
    return low + 256.0 * middle + 65536.0 * high


def code_columns(parts, triangle):
    return joined(matmul(triangle, parts, NT), 1)


def code_rows(parts, triangle):
    return joined(matmul(parts, triangle, NT), 0)


def exponent_row(rate_ref, heads, blocks):
    lane = lax.broadcasted_iota(jnp.int32, (1, blocks * heads), 1)
    row = jnp.zeros((1, blocks * heads), jnp.float32)
    for h in range(heads):
        row = jnp.where(lax.rem(lane, heads) == h, rate_ref[h], row)
    return row * (-1.0 / (CODE_SCALE * math.log(2.0)))


def head_lanes(row, start, heads):
    return jnp.concatenate(
        [jnp.broadcast_to(row[:, start + h : start + h + 1], (1, LANES)) for h in range(heads)], axis=1
    )


def summary_kernel(
    heads,
    blocks,
    rate_hbm,
    codes_hbm,
    write_hbm,
    x_hbm,
    piece_ref,
    local_ref,
    rate_ref,
    codes_ref,
    write_ref,
    x_ref,
    small_sem,
    write_sem,
    x_sem,
):
    small = [
        pltpu.make_async_copy(rate_hbm, rate_ref, small_sem.at[0]),
        pltpu.make_async_copy(codes_hbm, codes_ref, small_sem.at[1]),
    ]
    parts_of = [pl.ds(k * GROUP, GROUP) for k in range(blocks)]
    writes = [
        pltpu.make_async_copy(write_hbm.at[rows], write_ref.at[rows], write_sem.at[k]) for k, rows in enumerate(parts_of)
    ]
    inputs = [pltpu.make_async_copy(x_hbm.at[rows], x_ref.at[rows], x_sem.at[k]) for k, rows in enumerate(parts_of)]
    for copy in small:
        copy.start()
    for k in range(blocks):
        writes[k].start()
        inputs[k].start()
    triangle = lower_triangle(GROUP).astype(jnp.float32).astype(jnp.bfloat16)
    for copy in small:
        copy.wait()
    sums = code_columns(code_parts(codes_ref[...], heads, blocks), triangle)
    scale = exponent_row(rate_ref, heads, blocks)
    ends = sums[GROUP - 1 : GROUP, :]
    tail = jnp.exp2((ends - sums) * scale)
    block_decay = jnp.exp2(ends * scale)
    state = None
    for k, rows in enumerate(parts_of):
        writes[k].wait()
        inputs[k].wait()
        weighted = jnp.concatenate(
            [
                (tail[:, k * heads + h : k * heads + h + 1] * x_ref[rows, h * LANES : (h + 1) * LANES].astype(jnp.float32))
                .astype(jnp.bfloat16)
                for h in range(heads)
            ],
            axis=1,
        )
        added = matmul(write_ref[rows, :], weighted, TN)
        if k:
            local_ref[k - 1] = state
            state = head_lanes(block_decay, k * heads, heads) * state + added
        else:
            state = added
    total = sum(ends[:, k * heads : (k + 1) * heads] for k in range(blocks))
    section_decay = jnp.exp2(total * scale[:, :heads])
    quarters = Z // heads
    for h in range(heads):
        decay = jnp.broadcast_to(section_decay[:, h : h + 1], (PIECE_ROWS - PIECE, LANES))
        for q in range(quarters):
            piece_ref[h * quarters + q, :PIECE, :] = state[q * PIECE : (q + 1) * PIECE, h * LANES : (h + 1) * LANES]
            piece_ref[h * quarters + q, PIECE:, :] = decay


def inner_kernel(
    heads, blocks, rate_ref, skip_ref, codes_ref, write_ref, read_ref, x_ref, gate_ref, base_ref, factor_ref, lead_ref
):
    causal = lower_triangle(GROUP)
    triangle = causal.astype(jnp.float32).astype(jnp.bfloat16)
    corner = lower_triangle(HALF)
    parts = code_parts(codes_ref[...], heads, blocks)
    columns = code_columns(parts, triangle)
    across = code_rows(parts, triangle)
    scale = exponent_row(rate_ref, heads, blocks)
    grown = jnp.exp2(columns * scale)
    ends = columns[GROUP - 1 : GROUP, :]
    before = jnp.zeros((1, heads), jnp.float32)
    for k in range(blocks):
        lead_ref[k : k + 1, :] = head_lanes(jnp.exp2(before * scale[:, :heads]), 0, heads)
        before = before + ends[:, k * heads : (k + 1) * heads]
    for k in range(blocks):
        rows = pl.ds(k * GROUP, GROUP)
        scores = matmul(read_ref[rows, :], write_ref[rows, :], NT)
        for h in range(heads):
            at = k * heads + h
            lanes = slice(h * LANES, (h + 1) * LANES)
            factor = scale[:, h : h + 1]
            column = columns[:, at : at + 1]
            row = across[at : at + 1, :]

            def mixed(t0, t1, s0, s1, masked):
                decay = jnp.exp2((column[t0:t1] - row[:, s0:s1]) * factor) * scores[t0:t1, s0:s1]
                if masked:
                    decay = jnp.where(corner, decay, 0.0)
                return decay.astype(jnp.bfloat16)

            x_part = x_ref[rows, lanes]
            upper = matmul(mixed(0, HALF, 0, HALF, True), x_part[:HALF])
            lower = jnp.concatenate(
                [mixed(HALF, GROUP, 0, HALF, False), mixed(HALF, GROUP, HALF, GROUP, True)], axis=1
            )
            inner = jnp.concatenate([upper, matmul(lower, x_part)], axis=0)
            gate = gate_ref[rows, lanes].astype(jnp.float32)
            silu = gate / (1.0 + jnp.exp(-gate))
            base_ref[rows, lanes] = (inner + skip_ref[h] * x_part.astype(jnp.float32)) * silu
            factor_ref[rows, lanes] = grown[:, at : at + 1] * silu


def scan_kernel(got_ref, prefix_ref, decay_ref, total_ref):
    state = jnp.zeros((PIECE, LANES), jnp.float32)
    decay = jnp.ones((PIECE_ROWS - PIECE, LANES), jnp.float32)
    for i in range(Z):
        prefix_ref[i] = state
        decay_ref[i] = decay
        step = got_ref[i, PIECE:, :]
        state = step[:1] * state + got_ref[i, :PIECE, :]
        decay = step * decay
    for j in range(Y):
        total_ref[j, :PIECE, :] = state
        total_ref[j, PIECE:, :] = decay


def join_kernel(totals_ref, prefix_ref, decay_ref, out_ref):
    mine = lax.axis_index("y")
    state = jnp.zeros((PIECE, LANES), jnp.float32)
    for j in range(Y - 1):
        state = jnp.where(j < mine, totals_ref[j, PIECE : PIECE + 1, :] * state + totals_ref[j, :PIECE, :], state)
    for i in range(Z):
        out_ref[i] = decay_ref[i, :1, :] * state + prefix_ref[i]


def carry_kernel(heads, blocks, entering_ref, local_ref, lead_ref, read_ref, base_ref, factor_ref, gated_ref, power_ref):
    quarters = Z // heads
    entering = jnp.concatenate(
        [
            jnp.concatenate([entering_ref[h * quarters + q] for q in range(quarters)], axis=0)
            for h in range(heads)
        ],
        axis=1,
    )
    sums = []
    for k in range(blocks):
        rows = pl.ds(k * GROUP, GROUP)
        state = lead_ref[k : k + 1, :] * entering + local_ref[k - 1] if k else entering
        read_out = matmul(read_ref[rows, :], state.astype(jnp.bfloat16))
        gated = base_ref[rows, :] + factor_ref[rows, :] * read_out
        gated_ref[rows, :] = gated
        squares = gated * gated
        squares = sum(squares[:, h * LANES : (h + 1) * LANES] for h in range(heads))
        for half in range(GROUP // LANES):
            sums.append(jnp.sum(squares[half * LANES : (half + 1) * LANES].T, axis=0, keepdims=True))
    sums = jnp.concatenate(sums, axis=0)
    for j in range(HEAD):
        power_ref[j] = sums


def norm_kernel(heads, power_ref, gain_ref, gated_ref, out_hbm, out_ref, out_sem):
    power = sum(power_ref[j] for j in range(HEAD)) * (1.0 / CHANNELS)
    scale = lax.rsqrt(power + EPS)
    copies = []
    for r in range(scale.shape[0]):
        rows = pl.ds(r * LANES, LANES)
        column = jnp.broadcast_to(scale[r : r + 1, :], (LANES, LANES)).T
        for h in range(heads):
            lanes = slice(h * LANES, (h + 1) * LANES)
            out_ref[rows, lanes] = (gated_ref[rows, lanes] * column * gain_ref[:, lanes]).astype(jnp.bfloat16)
        copies.append(pltpu.make_async_copy(out_ref.at[rows], out_hbm.at[rows], out_sem.at[r]))
        copies[-1].start()
    for copy in copies:
        copy.wait()


VMEM = pl.BlockSpec(memory_space=pltpu.VMEM)
SMEM = pl.BlockSpec(memory_space=pltpu.SMEM)
HBM = pl.BlockSpec(memory_space=pltpu.HBM)


def call(kernel, out_shapes, in_specs, limit, flops, moved, scratch=(), out_spec=VMEM):
    return pl.pallas_call(
        kernel,
        out_shape=tuple(jax.ShapeDtypeStruct(shape, dtype) for shape, dtype in out_shapes),
        in_specs=in_specs,
        out_specs=tuple(out_spec for _ in out_shapes),
        scratch_shapes=scratch,
        compiler_params=pltpu.CompilerParams(vmem_limit_bytes=limit),
        cost_estimate=pl.CostEstimate(flops=flops, bytes_accessed=moved, transcendentals=0),
    )


def local(ssm_input, gate_input, write_proj, read_proj, decay_codes, decay_rate, skip_gain, norm_gain):
    rows, width = ssm_input.shape
    heads = decay_rate.shape[0]
    blocks = rows // GROUP
    f32 = jnp.float32
    piece, own = call(
        functools.partial(summary_kernel, heads, blocks),
        (((Z, PIECE_ROWS, LANES), f32), ((blocks - 1, LANES, width), f32)),
        [HBM] * 4,
        8 * MIB,
        1 << 28,
        3 * MIB,
        (
            pltpu.SMEM(decay_rate.shape, f32),
            pltpu.VMEM(decay_codes.shape, jnp.int32),
            pltpu.VMEM(write_proj.shape, jnp.bfloat16),
            pltpu.VMEM(ssm_input.shape, jnp.bfloat16),
            pltpu.SemaphoreType.DMA((2,)),
            pltpu.SemaphoreType.DMA((blocks,)),
            pltpu.SemaphoreType.DMA((blocks,)),
        ),
    )(*(pltpu.with_memory_space_constraint(a, pltpu.HBM) for a in (decay_rate, decay_codes, write_proj, ssm_input)))
    got = lax.all_to_all(piece, "z", 0, 0, tiled=True)
    base, factor, lead = call(
        functools.partial(inner_kernel, heads, blocks),
        (((rows, width), f32), ((rows, width), f32), ((blocks, width), f32)),
        [SMEM, SMEM, VMEM, VMEM, VMEM, VMEM, VMEM],
        24 * MIB,
        1 << 30,
        7 * MIB,
    )(decay_rate, skip_gain, decay_codes, write_proj, read_proj, ssm_input, gate_input)
    got, base, factor, lead = lax.optimization_barrier((got, base, factor, lead))
    prefix, prefix_decay, total = call(
        scan_kernel,
        (((Z, PIECE, LANES), f32), ((Z, PIECE_ROWS - PIECE, LANES), f32), ((Y, PIECE_ROWS, LANES), f32)),
        [VMEM],
        8 * MIB,
        1 << 33,
        MIB,
    )(got)
    totals = lax.all_to_all(total, "y", 0, 0, tiled=True)
    (joint,) = call(
        join_kernel, (((Z, PIECE, LANES), f32),), [VMEM, VMEM, VMEM], 8 * MIB, 1 << 33, MIB
    )(totals, prefix, prefix_decay)
    entering = lax.all_to_all(joint, "z", 0, 0, tiled=True)
    gated, power = call(
        functools.partial(carry_kernel, heads, blocks),
        (((rows, width), f32), ((HEAD, rows // LANES, LANES), f32)),
        [VMEM] * 6,
        16 * MIB,
        1 << 28,
        8 * MIB,
    )(entering, own, lead, read_proj, base, factor)
    powers = lax.all_to_all(power, "head", 0, 0, tiled=True)
    (out,) = call(
        functools.partial(norm_kernel, heads),
        (((rows, width), jnp.bfloat16),),
        [VMEM] * 3,
        8 * MIB,
        1 << 20,
        3 * MIB,
        (pltpu.VMEM((rows, width), jnp.bfloat16), pltpu.SemaphoreType.DMA((rows // LANES,))),
        HBM,
    )(powers, norm_gain.reshape(1, width), gated)
    return out


def solution(mesh):
    split = Mesh(mesh.devices.reshape(Y, Z, HEAD), ("y", "z", "head"))
    seq = ("y", "z")
    placed = (
        P(seq, "head"),
        P(seq, "head"),
        P(seq, None),
        P(seq, None),
        P("head", seq),
        P("head"),
        P("head"),
        P("head"),
    )
    return jax.shard_map(local, mesh=split, in_specs=placed, out_specs=P(seq, "head"), check_vma=False)
```

```python
import functools
import math

import jax
import jax.numpy as jnp
from jax import lax
from jax.experimental import pallas as pl
from jax.experimental.pallas import tpu as pltpu
from jax.sharding import Mesh
from jax.sharding import PartitionSpec as P

GROUP = 256
HALF = 128
LANES = 128
CODE_SCALE = 524288.0
CHANNELS = 4096
EPS = 1e-05
Y, FAR, NEAR, HEAD = 4, 4, 4, 8
STATE = 128
PIECE_ROWS = 136
MIB = 1 << 20
NT = (((1,), (1,)), ((), ()))
TN = (((0,), (0,)), ((), ()))


def matmul(a, b, dims=(((1,), (0,)), ((), ()))):
    return lax.dot_general(a, b, dims, preferred_element_type=jnp.float32)


def lower_triangle(size):
    row = lax.broadcasted_iota(jnp.int32, (size, size), 0)
    column = lax.broadcasted_iota(jnp.int32, (size, size), 1)
    return row >= column


def code_parts(codes, heads, blocks):
    rows = jnp.concatenate([codes[:, k * GROUP : (k + 1) * GROUP] for k in range(blocks)], axis=0)
    parts = [rows & 255, (rows >> 8) & 255, rows >> 16]
    return jnp.concatenate([part.astype(jnp.float32) for part in parts], axis=0).astype(jnp.bfloat16)


def joined(sums, axis):
    count = sums.shape[axis] // 3
    low, middle, high = (lax.slice_in_dim(sums, i * count, (i + 1) * count, axis=axis) for i in range(3))
    return low + 256.0 * middle + 65536.0 * high


def code_columns(parts, triangle):
    return joined(matmul(triangle, parts, NT), 1)


def code_rows(parts, triangle):
    return joined(matmul(parts, triangle, NT), 0)


def exponent_row(rate_ref, heads, blocks):
    lane = lax.broadcasted_iota(jnp.int32, (1, blocks * heads), 1)
    row = jnp.zeros((1, blocks * heads), jnp.float32)
    for h in range(heads):
        row = jnp.where(lax.rem(lane, heads) == h, rate_ref[h], row)
    return row * (-1.0 / (CODE_SCALE * math.log(2.0)))


def head_lanes(row, start, heads):
    return jnp.concatenate(
        [jnp.broadcast_to(row[:, start + h : start + h + 1], (1, LANES)) for h in range(heads)], axis=1
    )


def summary_kernel(
    heads,
    blocks,
    rate_hbm,
    codes_hbm,
    write_hbm,
    x_hbm,
    piece_ref,
    local_ref,
    rate_ref,
    codes_ref,
    write_ref,
    x_ref,
    small_sem,
    write_sem,
    x_sem,
):
    small = [
        pltpu.make_async_copy(rate_hbm, rate_ref, small_sem.at[0]),
        pltpu.make_async_copy(codes_hbm, codes_ref, small_sem.at[1]),
    ]
    parts_of = [pl.ds(k * GROUP, GROUP) for k in range(blocks)]
    writes = [
        pltpu.make_async_copy(write_hbm.at[rows], write_ref.at[rows], write_sem.at[k]) for k, rows in enumerate(parts_of)
    ]
    inputs = [pltpu.make_async_copy(x_hbm.at[rows], x_ref.at[rows], x_sem.at[k]) for k, rows in enumerate(parts_of)]
    for copy in small:
        copy.start()
    for k in range(blocks):
        writes[k].start()
        inputs[k].start()
    triangle = lower_triangle(GROUP).astype(jnp.float32).astype(jnp.bfloat16)
    for copy in small:
        copy.wait()
    sums = code_columns(code_parts(codes_ref[...], heads, blocks), triangle)
    scale = exponent_row(rate_ref, heads, blocks)
    ends = sums[GROUP - 1 : GROUP, :]
    tail = jnp.exp2((ends - sums) * scale)
    block_decay = jnp.exp2(ends * scale)
    state = None
    for k, rows in enumerate(parts_of):
        writes[k].wait()
        inputs[k].wait()
        weighted = jnp.concatenate(
            [
                (tail[:, k * heads + h : k * heads + h + 1] * x_ref[rows, h * LANES : (h + 1) * LANES].astype(jnp.float32))
                .astype(jnp.bfloat16)
                for h in range(heads)
            ],
            axis=1,
        )
        added = matmul(write_ref[rows, :], weighted, TN)
        if k:
            local_ref[k - 1] = state
            state = head_lanes(block_decay, k * heads, heads) * state + added
        else:
            state = added
    total = sum(ends[:, k * heads : (k + 1) * heads] for k in range(blocks))
    section_decay = jnp.exp2(total * scale[:, :heads])
    for h in range(heads):
        piece_ref[h, :STATE, :] = state[:, h * LANES : (h + 1) * LANES]
        piece_ref[h, STATE:, :] = jnp.broadcast_to(section_decay[:, h : h + 1], (PIECE_ROWS - STATE, LANES))


def inner_kernel(
    heads,
    blocks,
    rate_hbm,
    skip_hbm,
    codes_hbm,
    write_hbm,
    read_hbm,
    x_hbm,
    gate_hbm,
    base_ref,
    factor_ref,
    lead_ref,
    rate_ref,
    skip_ref,
    codes_ref,
    write_ref,
    read_ref,
    x_ref,
    gate_ref,
    sem,
):
    sources = (rate_hbm, skip_hbm, codes_hbm, write_hbm, read_hbm, x_hbm, gate_hbm)
    targets = (rate_ref, skip_ref, codes_ref, write_ref, read_ref, x_ref, gate_ref)
    copies = [pltpu.make_async_copy(a, b, sem.at[i]) for i, (a, b) in enumerate(zip(sources, targets, strict=True))]
    for copy in copies:
        copy.start()
    for copy in copies:
        copy.wait()
    causal = lower_triangle(GROUP)
    triangle = causal.astype(jnp.float32).astype(jnp.bfloat16)
    corner = lower_triangle(HALF)
    parts = code_parts(codes_ref[...], heads, blocks)
    columns = code_columns(parts, triangle)
    across = code_rows(parts, triangle)
    scale = exponent_row(rate_ref, heads, blocks)
    grown = jnp.exp2(columns * scale)
    ends = columns[GROUP - 1 : GROUP, :]
    before = jnp.zeros((1, heads), jnp.float32)
    for k in range(blocks):
        lead_ref[k : k + 1, :] = head_lanes(jnp.exp2(before * scale[:, :heads]), 0, heads)
        before = before + ends[:, k * heads : (k + 1) * heads]
    for k in range(blocks):
        rows = pl.ds(k * GROUP, GROUP)
        scores = matmul(read_ref[rows, :], write_ref[rows, :], NT)
        for h in range(heads):
            at = k * heads + h
            lanes = slice(h * LANES, (h + 1) * LANES)
            factor = scale[:, h : h + 1]
            column = columns[:, at : at + 1]
            row = across[at : at + 1, :]

            def mixed(t0, t1, s0, s1, masked):
                decay = jnp.exp2((column[t0:t1] - row[:, s0:s1]) * factor) * scores[t0:t1, s0:s1]
                if masked:
                    decay = jnp.where(corner, decay, 0.0)
                return decay.astype(jnp.bfloat16)

            x_part = x_ref[rows, lanes]
            upper = matmul(mixed(0, HALF, 0, HALF, True), x_part[:HALF])
            lower = jnp.concatenate(
                [mixed(HALF, GROUP, 0, HALF, False), mixed(HALF, GROUP, HALF, GROUP, True)], axis=1
            )
            inner = jnp.concatenate([upper, matmul(lower, x_part)], axis=0)
            gate = gate_ref[rows, lanes].astype(jnp.float32)
            silu = gate / (1.0 + jnp.exp(-gate))
            base_ref[rows, lanes] = (inner + skip_ref[h] * x_part.astype(jnp.float32)) * silu
            factor_ref[rows, lanes] = grown[:, at : at + 1] * silu


def near_kernel(got_ref, prefix_ref, decay_ref, total_ref):
    state = jnp.zeros((STATE, LANES), jnp.float32)
    decay = jnp.ones((PIECE_ROWS - STATE, LANES), jnp.float32)
    for i in range(NEAR):
        prefix_ref[i] = state
        decay_ref[i] = decay
        step = got_ref[i, STATE:, :]
        state = step[:1] * state + got_ref[i, :STATE, :]
        decay = step * decay
    for j in range(FAR):
        total_ref[j, :STATE, :] = state
        total_ref[j, STATE:, :] = decay


def far_kernel(got_ref, prefix_ref, total_ref):
    mine = lax.axis_index("far")
    state = jnp.zeros((STATE, LANES), jnp.float32)
    decay = jnp.ones((PIECE_ROWS - STATE, LANES), jnp.float32)
    own, own_decay = state, decay
    for i in range(FAR):
        own = jnp.where(i == mine, state, own)
        own_decay = jnp.where(i == mine, decay, own_decay)
        step = got_ref[i, STATE:, :]
        state = step[:1] * state + got_ref[i, :STATE, :]
        decay = step * decay
    prefix_ref[:STATE, :] = own
    prefix_ref[STATE:, :] = own_decay
    for j in range(Y):
        total_ref[j, :STATE, :] = state
        total_ref[j, STATE:, :] = decay


def join_kernel(totals_ref, group_ref, prefix_ref, decay_ref, out_ref):
    mine = lax.axis_index("y")
    state = jnp.zeros((STATE, LANES), jnp.float32)
    for j in range(Y - 1):
        state = jnp.where(j < mine, totals_ref[j, STATE : STATE + 1, :] * state + totals_ref[j, :STATE, :], state)
    state = group_ref[STATE : STATE + 1, :] * state + group_ref[:STATE, :]
    for i in range(NEAR):
        out_ref[i] = decay_ref[i, :1, :] * state + prefix_ref[i]


def carry_kernel(heads, blocks, entering_ref, local_ref, lead_ref, read_ref, base_ref, factor_ref, gated_ref, power_ref):
    entering = jnp.concatenate([entering_ref[h] for h in range(heads)], axis=1)
    sums = []
    for k in range(blocks):
        rows = pl.ds(k * GROUP, GROUP)
        state = lead_ref[k : k + 1, :] * entering + local_ref[k - 1] if k else entering
        read_out = matmul(read_ref[rows, :], state.astype(jnp.bfloat16))
        gated = base_ref[rows, :] + factor_ref[rows, :] * read_out
        gated_ref[rows, :] = gated
        squares = gated * gated
        squares = sum(squares[:, h * LANES : (h + 1) * LANES] for h in range(heads))
        for half in range(GROUP // LANES):
            sums.append(jnp.sum(squares[half * LANES : (half + 1) * LANES].T, axis=0, keepdims=True))
    sums = jnp.concatenate(sums, axis=0)
    for j in range(HEAD):
        power_ref[j] = sums


def norm_kernel(heads, power_ref, gain_ref, gated_ref, out_hbm, out_ref, out_sem):
    power = sum(power_ref[j] for j in range(HEAD)) * (1.0 / CHANNELS)
    scale = lax.rsqrt(power + EPS)
    copies = []
    for r in range(scale.shape[0]):
        rows = pl.ds(r * LANES, LANES)
        column = jnp.broadcast_to(scale[r : r + 1, :], (LANES, LANES)).T
        for h in range(heads):
            lanes = slice(h * LANES, (h + 1) * LANES)
            out_ref[rows, lanes] = (gated_ref[rows, lanes] * column * gain_ref[:, lanes]).astype(jnp.bfloat16)
        copies.append(pltpu.make_async_copy(out_ref.at[rows], out_hbm.at[rows], out_sem.at[r]))
        copies[-1].start()
    for copy in copies:
        copy.wait()


VMEM = pl.BlockSpec(memory_space=pltpu.VMEM)
SMEM = pl.BlockSpec(memory_space=pltpu.SMEM)
HBM = pl.BlockSpec(memory_space=pltpu.HBM)


def call(kernel, out_shapes, in_specs, limit, flops, moved, scratch=(), out_spec=VMEM):
    return pl.pallas_call(
        kernel,
        out_shape=tuple(jax.ShapeDtypeStruct(shape, dtype) for shape, dtype in out_shapes),
        in_specs=in_specs,
        out_specs=tuple(out_spec for _ in out_shapes),
        scratch_shapes=scratch,
        compiler_params=pltpu.CompilerParams(vmem_limit_bytes=limit),
        cost_estimate=pl.CostEstimate(flops=flops, bytes_accessed=moved, transcendentals=0),
    )


def in_hbm(*arrays):
    return tuple(pltpu.with_memory_space_constraint(array, pltpu.HBM) for array in arrays)


def local(ssm_input, gate_input, write_proj, read_proj, decay_codes, decay_rate, skip_gain, norm_gain):
    rows, width = ssm_input.shape
    heads = decay_rate.shape[0]
    blocks = rows // GROUP
    f32, bf16 = jnp.float32, jnp.bfloat16
    piece, own = call(
        functools.partial(summary_kernel, heads, blocks),
        (((NEAR, PIECE_ROWS, LANES), f32), ((blocks - 1, LANES, width), f32)),
        [HBM] * 4,
        8 * MIB,
        1 << 28,
        3 * MIB,
        (
            pltpu.SMEM(decay_rate.shape, f32),
            pltpu.VMEM(decay_codes.shape, jnp.int32),
            pltpu.VMEM(write_proj.shape, bf16),
            pltpu.VMEM(ssm_input.shape, bf16),
            pltpu.SemaphoreType.DMA((2,)),
            pltpu.SemaphoreType.DMA((blocks,)),
            pltpu.SemaphoreType.DMA((blocks,)),
        ),
    )(*in_hbm(decay_rate, decay_codes, write_proj, ssm_input))
    got = lax.all_to_all(piece, "near", 0, 0, tiled=True)
    got, later_gate = lax.optimization_barrier((got, gate_input))
    prefix, prefix_decay, total = call(
        near_kernel,
        (((NEAR, STATE, LANES), f32), ((NEAR, PIECE_ROWS - STATE, LANES), f32), ((FAR, PIECE_ROWS, LANES), f32)),
        [VMEM],
        8 * MIB,
        1 << 20,
        MIB,
    )(got)
    totals = lax.all_to_all(total, "far", 0, 0, tiled=True)
    base, factor, lead = call(
        functools.partial(inner_kernel, heads, blocks),
        (((rows, width), f32), ((rows, width), f32), ((blocks, width), f32)),
        [HBM] * 7,
        16 * MIB,
        1 << 30,
        7 * MIB,
        (
            pltpu.SMEM(decay_rate.shape, f32),
            pltpu.SMEM(skip_gain.shape, f32),
            pltpu.VMEM(decay_codes.shape, jnp.int32),
            pltpu.VMEM(write_proj.shape, bf16),
            pltpu.VMEM(read_proj.shape, bf16),
            pltpu.VMEM(ssm_input.shape, bf16),
            pltpu.VMEM(gate_input.shape, bf16),
            pltpu.SemaphoreType.DMA((7,)),
        ),
    )(*in_hbm(decay_rate, skip_gain, decay_codes, write_proj, read_proj, ssm_input, later_gate))
    totals, base, factor, lead = lax.optimization_barrier((totals, base, factor, lead))
    group, row_total = call(
        far_kernel,
        (((PIECE_ROWS, LANES), f32), ((Y, PIECE_ROWS, LANES), f32)),
        [VMEM],
        8 * MIB,
        1 << 33,
        MIB,
    )(totals)
    row_totals = lax.all_to_all(row_total, "y", 0, 0, tiled=True)
    (joint,) = call(join_kernel, (((NEAR, STATE, LANES), f32),), [VMEM] * 4, 8 * MIB, 1 << 33, MIB)(
        row_totals, group, prefix, prefix_decay
    )
    entering = lax.all_to_all(joint, "near", 0, 0, tiled=True)
    gated, power = call(
        functools.partial(carry_kernel, heads, blocks),
        (((rows, width), f32), ((HEAD, rows // LANES, LANES), f32)),
        [VMEM] * 6,
        16 * MIB,
        1 << 28,
        8 * MIB,
    )(entering, own, lead, read_proj, base, factor)
    powers = lax.all_to_all(power, "head", 0, 0, tiled=True)
    (out,) = call(
        functools.partial(norm_kernel, heads),
        (((rows, width), bf16),),
        [VMEM] * 3,
        8 * MIB,
        1 << 20,
        3 * MIB,
        (pltpu.VMEM((rows, width), bf16), pltpu.SemaphoreType.DMA((rows // LANES,))),
        HBM,
    )(powers, norm_gain.reshape(1, width), gated)
    return out


def solution(mesh):
    split = Mesh(mesh.devices.reshape(Y, FAR, NEAR, HEAD), ("y", "far", "near", "head"))
    seq = ("y", "far", "near")
    placed = (
        P(seq, "head"),
        P(seq, "head"),
        P(seq, None),
        P(seq, None),
        P("head", seq),
        P("head"),
        P("head"),
        P("head"),
    )
    return jax.shard_map(local, mesh=split, in_specs=placed, out_specs=P(seq, "head"), check_vma=False)
```

```python
import functools
import math

import jax
import jax.numpy as jnp
from jax import lax
from jax.experimental import pallas as pl
from jax.experimental.pallas import tpu as pltpu
from jax.sharding import Mesh
from jax.sharding import PartitionSpec as P

GROUP = 256
HALF = 128
LANES = 128
CODE_SCALE = 524288.0
CHANNELS = 4096
EPS = 1e-05
Y, FAR, NEAR, HEAD = 4, 4, 4, 8
STATE = 128
PIECE_ROWS = 136
MIB = 1 << 20
NT = (((1,), (1,)), ((), ()))
TN = (((0,), (0,)), ((), ()))


def matmul(a, b, dims=(((1,), (0,)), ((), ()))):
    return lax.dot_general(a, b, dims, preferred_element_type=jnp.float32)


def lower_triangle(size):
    row = lax.broadcasted_iota(jnp.int32, (size, size), 0)
    column = lax.broadcasted_iota(jnp.int32, (size, size), 1)
    return row >= column


def code_parts(codes, heads, blocks):
    rows = jnp.concatenate([codes[:, k * GROUP : (k + 1) * GROUP] for k in range(blocks)], axis=0)
    parts = [rows & 255, (rows >> 8) & 255, rows >> 16]
    return jnp.concatenate([part.astype(jnp.float32) for part in parts], axis=0).astype(jnp.bfloat16)


def joined(sums, axis):
    count = sums.shape[axis] // 3
    low, middle, high = (lax.slice_in_dim(sums, i * count, (i + 1) * count, axis=axis) for i in range(3))
    return low + 256.0 * middle + 65536.0 * high


def code_columns(parts, triangle):
    return joined(matmul(triangle, parts, NT), 1)


def code_rows(parts, triangle):
    return joined(matmul(parts, triangle, NT), 0)


def exponent_row(rate_ref, heads, blocks):
    lane = lax.broadcasted_iota(jnp.int32, (1, blocks * heads), 1)
    row = jnp.zeros((1, blocks * heads), jnp.float32)
    for h in range(heads):
        row = jnp.where(lax.rem(lane, heads) == h, rate_ref[h], row)
    return row * (-1.0 / (CODE_SCALE * math.log(2.0)))


def head_lanes(row, start, heads):
    return jnp.concatenate(
        [jnp.broadcast_to(row[:, start + h : start + h + 1], (1, LANES)) for h in range(heads)], axis=1
    )


def weighted_inputs(tail, x_ref, rows, k, heads):
    return jnp.concatenate(
        [
            (tail[:, k * heads + h : k * heads + h + 1] * x_ref[rows, h * LANES : (h + 1) * LANES].astype(jnp.float32))
            .astype(jnp.bfloat16)
            for h in range(heads)
        ],
        axis=1,
    )


def summary_kernel(
    heads,
    blocks,
    rate_hbm,
    codes_hbm,
    write_hbm,
    x_hbm,
    piece_ref,
    rate_ref,
    codes_ref,
    write_ref,
    x_ref,
    sem,
):
    pairs = ((rate_hbm, rate_ref), (codes_hbm, codes_ref), (write_hbm, write_ref), (x_hbm, x_ref))
    copies = [pltpu.make_async_copy(a, b, sem.at[i]) for i, (a, b) in enumerate(pairs)]
    for copy in copies:
        copy.start()
    triangle = lower_triangle(GROUP).astype(jnp.float32).astype(jnp.bfloat16)
    for copy in copies[:2]:
        copy.wait()
    sums = code_columns(code_parts(codes_ref[...], heads, blocks), triangle)
    scale = exponent_row(rate_ref, heads, blocks)
    ends = sums[GROUP - 1 : GROUP, :]
    to_end = [ends[:, (blocks - 1) * heads :]]
    for k in range(blocks - 2, -1, -1):
        to_end.insert(0, ends[:, k * heads : (k + 1) * heads] + to_end[0])
    section_decay = jnp.exp2(to_end[0] * scale[:, :heads])
    tail = jnp.exp2((jnp.concatenate(to_end, axis=1) - sums) * scale)
    for copy in copies[2:]:
        copy.wait()
    state = None
    for k in range(blocks):
        rows = pl.ds(k * GROUP, GROUP)
        added = matmul(write_ref[rows, :], weighted_inputs(tail, x_ref, rows, k, heads), TN)
        state = state + added if k else added
    for h in range(heads):
        piece_ref[h, :STATE, :] = state[:, h * LANES : (h + 1) * LANES]
        piece_ref[h, STATE:, :] = jnp.broadcast_to(section_decay[:, h : h + 1], (PIECE_ROWS - STATE, LANES))


def inner_kernel(
    heads,
    blocks,
    rate_hbm,
    skip_hbm,
    codes_hbm,
    write_hbm,
    read_hbm,
    x_hbm,
    gate_hbm,
    base_ref,
    factor_ref,
    lead_ref,
    local_ref,
    rate_ref,
    skip_ref,
    codes_ref,
    write_ref,
    read_ref,
    x_ref,
    gate_ref,
    sem,
):
    sources = (rate_hbm, skip_hbm, codes_hbm, write_hbm, read_hbm, x_hbm, gate_hbm)
    targets = (rate_ref, skip_ref, codes_ref, write_ref, read_ref, x_ref, gate_ref)
    copies = [pltpu.make_async_copy(a, b, sem.at[i]) for i, (a, b) in enumerate(zip(sources, targets, strict=True))]
    for copy in copies:
        copy.start()
    for copy in copies:
        copy.wait()
    causal = lower_triangle(GROUP)
    triangle = causal.astype(jnp.float32).astype(jnp.bfloat16)
    corner = lower_triangle(HALF)
    parts = code_parts(codes_ref[...], heads, blocks)
    columns = code_columns(parts, triangle)
    across = code_rows(parts, triangle)
    scale = exponent_row(rate_ref, heads, blocks)
    grown = jnp.exp2(columns * scale)
    ends = columns[GROUP - 1 : GROUP, :]
    tail = jnp.exp2((ends - columns) * scale)
    block_decay = jnp.exp2(ends * scale)
    state = None
    for k in range(blocks - 1):
        rows = pl.ds(k * GROUP, GROUP)
        added = matmul(write_ref[rows, :], weighted_inputs(tail, x_ref, rows, k, heads), TN)
        state = head_lanes(block_decay, k * heads, heads) * state + added if k else added
        local_ref[k] = state
    before = jnp.zeros((1, heads), jnp.float32)
    for k in range(blocks):
        lead_ref[k : k + 1, :] = head_lanes(jnp.exp2(before * scale[:, :heads]), 0, heads)
        before = before + ends[:, k * heads : (k + 1) * heads]
    for k in range(blocks):
        rows = pl.ds(k * GROUP, GROUP)
        scores = matmul(read_ref[rows, :], write_ref[rows, :], NT)
        for h in range(heads):
            at = k * heads + h
            lanes = slice(h * LANES, (h + 1) * LANES)
            factor = scale[:, h : h + 1]
            column = columns[:, at : at + 1]
            row = across[at : at + 1, :]

            def mixed(t0, t1, s0, s1, masked):
                decay = jnp.exp2((column[t0:t1] - row[:, s0:s1]) * factor) * scores[t0:t1, s0:s1]
                if masked:
                    decay = jnp.where(corner, decay, 0.0)
                return decay.astype(jnp.bfloat16)

            x_part = x_ref[rows, lanes]
            upper = matmul(mixed(0, HALF, 0, HALF, True), x_part[:HALF])
            lower = jnp.concatenate(
                [mixed(HALF, GROUP, 0, HALF, False), mixed(HALF, GROUP, HALF, GROUP, True)], axis=1
            )
            inner = jnp.concatenate([upper, matmul(lower, x_part)], axis=0)
            gate = gate_ref[rows, lanes].astype(jnp.float32)
            silu = gate / (1.0 + jnp.exp(-gate))
            base_ref[rows, lanes] = (inner + skip_ref[h] * x_part.astype(jnp.float32)) * silu
            factor_ref[rows, lanes] = grown[:, at : at + 1] * silu


def near_kernel(got_ref, prefix_ref, decay_ref, total_ref):
    state = jnp.zeros((STATE, LANES), jnp.float32)
    decay = jnp.ones((PIECE_ROWS - STATE, LANES), jnp.float32)
    for i in range(NEAR):
        prefix_ref[i] = state
        decay_ref[i] = decay
        step = got_ref[i, STATE:, :]
        state = step[:1] * state + got_ref[i, :STATE, :]
        decay = step * decay
    for j in range(FAR):
        total_ref[j, :STATE, :] = state
        total_ref[j, STATE:, :] = decay


def far_kernel(got_ref, prefix_ref, total_ref):
    mine = lax.axis_index("far")
    state = jnp.zeros((STATE, LANES), jnp.float32)
    decay = jnp.ones((PIECE_ROWS - STATE, LANES), jnp.float32)
    own, own_decay = state, decay
    for i in range(FAR):
        own = jnp.where(i == mine, state, own)
        own_decay = jnp.where(i == mine, decay, own_decay)
        step = got_ref[i, STATE:, :]
        state = step[:1] * state + got_ref[i, :STATE, :]
        decay = step * decay
    prefix_ref[:STATE, :] = own
    prefix_ref[STATE:, :] = own_decay
    for j in range(Y):
        total_ref[j, :STATE, :] = state
        total_ref[j, STATE:, :] = decay


def join_kernel(totals_ref, group_ref, prefix_ref, decay_ref, out_ref):
    mine = lax.axis_index("y")
    state = jnp.zeros((STATE, LANES), jnp.float32)
    for j in range(Y - 1):
        state = jnp.where(j < mine, totals_ref[j, STATE : STATE + 1, :] * state + totals_ref[j, :STATE, :], state)
    state = group_ref[STATE : STATE + 1, :] * state + group_ref[:STATE, :]
    for i in range(NEAR):
        out_ref[i] = decay_ref[i, :1, :] * state + prefix_ref[i]


def carry_kernel(heads, blocks, entering_ref, local_ref, lead_ref, read_ref, base_ref, factor_ref, gated_ref, power_ref):
    entering = jnp.concatenate([entering_ref[h] for h in range(heads)], axis=1)
    sums = []
    for k in range(blocks):
        rows = pl.ds(k * GROUP, GROUP)
        state = lead_ref[k : k + 1, :] * entering + local_ref[k - 1] if k else entering
        read_out = matmul(read_ref[rows, :], state.astype(jnp.bfloat16))
        gated = base_ref[rows, :] + factor_ref[rows, :] * read_out
        gated_ref[rows, :] = gated
        squares = gated * gated
        squares = sum(squares[:, h * LANES : (h + 1) * LANES] for h in range(heads))
        for half in range(GROUP // LANES):
            sums.append(jnp.sum(squares[half * LANES : (half + 1) * LANES].T, axis=0, keepdims=True))
    sums = jnp.concatenate(sums, axis=0)
    for j in range(HEAD):
        power_ref[j] = sums


def norm_kernel(heads, power_ref, gain_ref, gated_ref, out_hbm, out_ref, out_sem):
    power = sum(power_ref[j] for j in range(HEAD)) * (1.0 / CHANNELS)
    scale = lax.rsqrt(power + EPS)
    copies = []
    for r in range(scale.shape[0]):
        rows = pl.ds(r * LANES, LANES)
        column = jnp.broadcast_to(scale[r : r + 1, :], (LANES, LANES)).T
        for h in range(heads):
            lanes = slice(h * LANES, (h + 1) * LANES)
            out_ref[rows, lanes] = (gated_ref[rows, lanes] * column * gain_ref[:, lanes]).astype(jnp.bfloat16)
        copies.append(pltpu.make_async_copy(out_ref.at[rows], out_hbm.at[rows], out_sem.at[r]))
        copies[-1].start()
    for copy in copies:
        copy.wait()


VMEM = pl.BlockSpec(memory_space=pltpu.VMEM)
SMEM = pl.BlockSpec(memory_space=pltpu.SMEM)
HBM = pl.BlockSpec(memory_space=pltpu.HBM)


def call(kernel, out_shapes, in_specs, limit, flops, moved, scratch=(), out_spec=VMEM):
    return pl.pallas_call(
        kernel,
        out_shape=tuple(jax.ShapeDtypeStruct(shape, dtype) for shape, dtype in out_shapes),
        in_specs=in_specs,
        out_specs=tuple(out_spec for _ in out_shapes),
        scratch_shapes=scratch,
        compiler_params=pltpu.CompilerParams(vmem_limit_bytes=limit),
        cost_estimate=pl.CostEstimate(flops=flops, bytes_accessed=moved, transcendentals=0),
    )


def in_hbm(*arrays):
    return tuple(pltpu.with_memory_space_constraint(array, pltpu.HBM) for array in arrays)


def local(ssm_input, gate_input, write_proj, read_proj, decay_codes, decay_rate, skip_gain, norm_gain):
    rows, width = ssm_input.shape
    heads = decay_rate.shape[0]
    blocks = rows // GROUP
    f32, bf16 = jnp.float32, jnp.bfloat16
    (piece,) = call(
        functools.partial(summary_kernel, heads, blocks),
        (((NEAR, PIECE_ROWS, LANES), f32),),
        [HBM] * 4,
        8 * MIB,
        1 << 28,
        3 * MIB,
        (
            pltpu.SMEM(decay_rate.shape, f32),
            pltpu.VMEM(decay_codes.shape, jnp.int32),
            pltpu.VMEM(write_proj.shape, bf16),
            pltpu.VMEM(ssm_input.shape, bf16),
            pltpu.SemaphoreType.DMA((4,)),
        ),
    )(*in_hbm(decay_rate, decay_codes, write_proj, ssm_input))
    got = lax.all_to_all(piece, "near", 0, 0, tiled=True)
    got, later_gate = lax.optimization_barrier((got, gate_input))
    prefix, prefix_decay, total = call(
        near_kernel,
        (((NEAR, STATE, LANES), f32), ((NEAR, PIECE_ROWS - STATE, LANES), f32), ((FAR, PIECE_ROWS, LANES), f32)),
        [VMEM],
        8 * MIB,
        1 << 20,
        MIB,
    )(got)
    totals = lax.all_to_all(total, "far", 0, 0, tiled=True)
    base, factor, lead, own = call(
        functools.partial(inner_kernel, heads, blocks),
        (((rows, width), f32), ((rows, width), f32), ((blocks, width), f32), ((blocks - 1, STATE, width), f32)),
        [HBM] * 7,
        16 * MIB,
        1 << 30,
        7 * MIB,
        (
            pltpu.SMEM(decay_rate.shape, f32),
            pltpu.SMEM(skip_gain.shape, f32),
            pltpu.VMEM(decay_codes.shape, jnp.int32),
            pltpu.VMEM(write_proj.shape, bf16),
            pltpu.VMEM(read_proj.shape, bf16),
            pltpu.VMEM(ssm_input.shape, bf16),
            pltpu.VMEM(gate_input.shape, bf16),
            pltpu.SemaphoreType.DMA((7,)),
        ),
    )(*in_hbm(decay_rate, skip_gain, decay_codes, write_proj, read_proj, ssm_input, later_gate))
    totals, base, factor, lead, own = lax.optimization_barrier((totals, base, factor, lead, own))
    group, row_total = call(
        far_kernel,
        (((PIECE_ROWS, LANES), f32), ((Y, PIECE_ROWS, LANES), f32)),
        [VMEM],
        8 * MIB,
        1 << 33,
        MIB,
    )(totals)
    row_totals = lax.all_to_all(row_total, "y", 0, 0, tiled=True)
    (joint,) = call(join_kernel, (((NEAR, STATE, LANES), f32),), [VMEM] * 4, 8 * MIB, 1 << 33, MIB)(
        row_totals, group, prefix, prefix_decay
    )
    entering = lax.all_to_all(joint, "near", 0, 0, tiled=True)
    gated, power = call(
        functools.partial(carry_kernel, heads, blocks),
        (((rows, width), f32), ((HEAD, rows // LANES, LANES), f32)),
        [VMEM] * 6,
        16 * MIB,
        1 << 28,
        8 * MIB,
    )(entering, own, lead, read_proj, base, factor)
    powers = lax.all_to_all(power, "head", 0, 0, tiled=True)
    (out,) = call(
        functools.partial(norm_kernel, heads),
        (((rows, width), bf16),),
        [VMEM] * 3,
        8 * MIB,
        1 << 20,
        3 * MIB,
        (pltpu.VMEM((rows, width), bf16), pltpu.SemaphoreType.DMA((rows // LANES,))),
        HBM,
    )(powers, norm_gain.reshape(1, width), gated)
    return out


def solution(mesh):
    split = Mesh(mesh.devices.reshape(Y, FAR, NEAR, HEAD), ("y", "far", "near", "head"))
    seq = ("y", "far", "near")
    placed = (
        P(seq, "head"),
        P(seq, "head"),
        P(seq, None),
        P(seq, None),
        P("head", seq),
        P("head"),
        P("head"),
        P("head"),
    )
    return jax.shard_map(local, mesh=split, in_specs=placed, out_specs=P(seq, "head"), check_vma=False)
```

```python
import functools
import math

import jax
import jax.numpy as jnp
from jax import lax
from jax.experimental import pallas as pl
from jax.experimental.pallas import tpu as pltpu
from jax.sharding import Mesh
from jax.sharding import PartitionSpec as P

GROUP = 256
HALF = 128
LANES = 128
CODE_SCALE = 524288.0
CHANNELS = 4096
EPS = 1e-05
Y, FAR, NEAR, HEAD = 4, 4, 4, 8
STATE = 128
PIECE_ROWS = 136
MIB = 1 << 20
NT = (((1,), (1,)), ((), ()))
TN = (((0,), (0,)), ((), ()))


def matmul(a, b, dims=(((1,), (0,)), ((), ()))):
    return lax.dot_general(a, b, dims, preferred_element_type=jnp.float32)


def lower_triangle(size):
    row = lax.broadcasted_iota(jnp.int32, (size, size), 0)
    column = lax.broadcasted_iota(jnp.int32, (size, size), 1)
    return row >= column


def code_parts(codes, heads, blocks):
    rows = jnp.concatenate([codes[:, k * GROUP : (k + 1) * GROUP] for k in range(blocks)], axis=0)
    parts = [rows & 255, (rows >> 8) & 255, rows >> 16]
    return jnp.concatenate([part.astype(jnp.float32) for part in parts], axis=0).astype(jnp.bfloat16)


def joined(sums, axis):
    count = sums.shape[axis] // 3
    low, middle, high = (lax.slice_in_dim(sums, i * count, (i + 1) * count, axis=axis) for i in range(3))
    return low + 256.0 * middle + 65536.0 * high


def code_columns(parts, triangle):
    return joined(matmul(triangle, parts, NT), 1)


def code_rows(parts, triangle):
    return joined(matmul(parts, triangle, NT), 0)


def exponent_row(rate_ref, heads, blocks):
    lane = lax.broadcasted_iota(jnp.int32, (1, blocks * heads), 1)
    row = jnp.zeros((1, blocks * heads), jnp.float32)
    for h in range(heads):
        row = jnp.where(lax.rem(lane, heads) == h, rate_ref[h], row)
    return row * (-1.0 / (CODE_SCALE * math.log(2.0)))


def head_lanes(row, start, heads):
    return jnp.concatenate(
        [jnp.broadcast_to(row[:, start + h : start + h + 1], (1, LANES)) for h in range(heads)], axis=1
    )


def weighted_inputs(tail, x_ref, rows, k, heads):
    return jnp.concatenate(
        [
            (tail[:, k * heads + h : k * heads + h + 1] * x_ref[rows, h * LANES : (h + 1) * LANES].astype(jnp.float32))
            .astype(jnp.bfloat16)
            for h in range(heads)
        ],
        axis=1,
    )


def summary_kernel(
    heads,
    blocks,
    rate_hbm,
    codes_hbm,
    write_hbm,
    x_hbm,
    piece_ref,
    rate_ref,
    codes_ref,
    write_ref,
    x_ref,
    sem,
):
    pairs = ((rate_hbm, rate_ref), (codes_hbm, codes_ref), (write_hbm, write_ref), (x_hbm, x_ref))
    copies = [pltpu.make_async_copy(a, b, sem.at[i]) for i, (a, b) in enumerate(pairs)]
    for copy in copies:
        copy.start()
    triangle = lower_triangle(GROUP).astype(jnp.float32).astype(jnp.bfloat16)
    for copy in copies[:2]:
        copy.wait()
    sums = code_columns(code_parts(codes_ref[...], heads, blocks), triangle)
    scale = exponent_row(rate_ref, heads, blocks)
    ends = sums[GROUP - 1 : GROUP, :]
    tail = jnp.exp2((ends - sums) * scale)
    block_decay = jnp.exp2(ends * scale)
    total = sum(ends[:, k * heads : (k + 1) * heads] for k in range(blocks))
    section_decay = jnp.exp2(total * scale[:, :heads])
    for copy in copies[2:]:
        copy.wait()
    state = None
    for k in range(blocks):
        rows = pl.ds(k * GROUP, GROUP)
        added = matmul(write_ref[rows, :], weighted_inputs(tail, x_ref, rows, k, heads), TN)
        state = head_lanes(block_decay, k * heads, heads) * state + added if k else added
    for h in range(heads):
        piece_ref[h, :STATE, :] = state[:, h * LANES : (h + 1) * LANES]
        piece_ref[h, STATE:, :] = jnp.broadcast_to(section_decay[:, h : h + 1], (PIECE_ROWS - STATE, LANES))


def inner_kernel(
    heads,
    blocks,
    rate_hbm,
    skip_hbm,
    codes_hbm,
    write_hbm,
    read_hbm,
    x_hbm,
    gate_hbm,
    base_ref,
    factor_ref,
    lead_ref,
    local_ref,
    rate_ref,
    skip_ref,
    codes_ref,
    write_ref,
    read_ref,
    x_ref,
    gate_ref,
    sem,
):
    sources = (rate_hbm, skip_hbm, codes_hbm, write_hbm, read_hbm, x_hbm, gate_hbm)
    targets = (rate_ref, skip_ref, codes_ref, write_ref, read_ref, x_ref, gate_ref)
    copies = [pltpu.make_async_copy(a, b, sem.at[i]) for i, (a, b) in enumerate(zip(sources, targets, strict=True))]
    for copy in copies:
        copy.start()
    for copy in copies:
        copy.wait()
    causal = lower_triangle(GROUP)
    triangle = causal.astype(jnp.float32).astype(jnp.bfloat16)
    corner = lower_triangle(HALF)
    parts = code_parts(codes_ref[...], heads, blocks)
    columns = code_columns(parts, triangle)
    across = code_rows(parts, triangle)
    scale = exponent_row(rate_ref, heads, blocks)
    grown = jnp.exp2(columns * scale)
    ends = columns[GROUP - 1 : GROUP, :]
    tail = jnp.exp2((ends - columns) * scale)
    block_decay = jnp.exp2(ends * scale)
    state = None
    for k in range(blocks - 1):
        rows = pl.ds(k * GROUP, GROUP)
        added = matmul(write_ref[rows, :], weighted_inputs(tail, x_ref, rows, k, heads), TN)
        state = head_lanes(block_decay, k * heads, heads) * state + added if k else added
        local_ref[k] = state
    before = jnp.zeros((1, heads), jnp.float32)
    for k in range(blocks):
        lead_ref[k : k + 1, :] = head_lanes(jnp.exp2(before * scale[:, :heads]), 0, heads)
        before = before + ends[:, k * heads : (k + 1) * heads]
    for k in range(blocks):
        rows = pl.ds(k * GROUP, GROUP)
        scores = matmul(read_ref[rows, :], write_ref[rows, :], NT)
        for h in range(heads):
            at = k * heads + h
            lanes = slice(h * LANES, (h + 1) * LANES)
            factor = scale[:, h : h + 1]
            column = columns[:, at : at + 1]
            row = across[at : at + 1, :]

            def mixed(t0, t1, s0, s1, masked):
                decay = jnp.exp2((column[t0:t1] - row[:, s0:s1]) * factor) * scores[t0:t1, s0:s1]
                if masked:
                    decay = jnp.where(corner, decay, 0.0)
                return decay.astype(jnp.bfloat16)

            x_part = x_ref[rows, lanes]
            upper = matmul(mixed(0, HALF, 0, HALF, True), x_part[:HALF])
            lower = jnp.concatenate(
                [mixed(HALF, GROUP, 0, HALF, False), mixed(HALF, GROUP, HALF, GROUP, True)], axis=1
            )
            inner = jnp.concatenate([upper, matmul(lower, x_part)], axis=0)
            gate = gate_ref[rows, lanes].astype(jnp.float32)
            silu = gate / (1.0 + jnp.exp(-gate))
            base_ref[rows, lanes] = (inner + skip_ref[h] * x_part.astype(jnp.float32)) * silu
            factor_ref[rows, lanes] = grown[:, at : at + 1] * silu


def near_kernel(got_ref, prefix_ref, decay_ref, total_ref):
    state = jnp.zeros((STATE, LANES), jnp.float32)
    decay = jnp.ones((PIECE_ROWS - STATE, LANES), jnp.float32)
    for i in range(NEAR):
        prefix_ref[i] = state
        decay_ref[i] = decay
        step = got_ref[i, STATE:, :]
        state = step[:1] * state + got_ref[i, :STATE, :]
        decay = step * decay
    for j in range(FAR):
        total_ref[j, :STATE, :] = state
        total_ref[j, STATE:, :] = decay


def far_kernel(got_ref, prefix_ref, total_ref):
    mine = lax.axis_index("far")
    state = jnp.zeros((STATE, LANES), jnp.float32)
    decay = jnp.ones((PIECE_ROWS - STATE, LANES), jnp.float32)
    own, own_decay = state, decay
    for i in range(FAR):
        own = jnp.where(i == mine, state, own)
        own_decay = jnp.where(i == mine, decay, own_decay)
        step = got_ref[i, STATE:, :]
        state = step[:1] * state + got_ref[i, :STATE, :]
        decay = step * decay
    prefix_ref[:STATE, :] = own
    prefix_ref[STATE:, :] = own_decay
    for j in range(Y):
        total_ref[j, :STATE, :] = state
        total_ref[j, STATE:, :] = decay


def join_kernel(totals_ref, group_ref, prefix_ref, decay_ref, out_ref):
    mine = lax.axis_index("y")
    state = jnp.zeros((STATE, LANES), jnp.float32)
    for j in range(Y - 1):
        state = jnp.where(j < mine, totals_ref[j, STATE : STATE + 1, :] * state + totals_ref[j, :STATE, :], state)
    state = group_ref[STATE : STATE + 1, :] * state + group_ref[:STATE, :]
    for i in range(NEAR):
        out_ref[i] = decay_ref[i, :1, :] * state + prefix_ref[i]


def carry_kernel(heads, blocks, entering_ref, local_ref, lead_ref, read_ref, base_ref, factor_ref, gated_ref, power_ref):
    entering = jnp.concatenate([entering_ref[h] for h in range(heads)], axis=1)
    sums = []
    for k in range(blocks):
        rows = pl.ds(k * GROUP, GROUP)
        state = lead_ref[k : k + 1, :] * entering + local_ref[k - 1] if k else entering
        read_out = matmul(read_ref[rows, :], state.astype(jnp.bfloat16))
        gated = base_ref[rows, :] + factor_ref[rows, :] * read_out
        gated_ref[rows, :] = gated
        squares = gated * gated
        squares = sum(squares[:, h * LANES : (h + 1) * LANES] for h in range(heads))
        for half in range(GROUP // LANES):
            sums.append(jnp.sum(squares[half * LANES : (half + 1) * LANES].T, axis=0, keepdims=True))
    sums = jnp.concatenate(sums, axis=0)
    for j in range(HEAD):
        power_ref[j] = sums


def norm_kernel(heads, power_ref, gain_ref, gated_ref, out_hbm, out_ref, out_sem):
    power = sum(power_ref[j] for j in range(HEAD)) * (1.0 / CHANNELS)
    scale = lax.rsqrt(power + EPS)
    copies = []
    for r in range(scale.shape[0]):
        rows = pl.ds(r * LANES, LANES)
        column = jnp.broadcast_to(scale[r : r + 1, :], (LANES, LANES)).T
        for h in range(heads):
            lanes = slice(h * LANES, (h + 1) * LANES)
            out_ref[rows, lanes] = (gated_ref[rows, lanes] * column * gain_ref[:, lanes]).astype(jnp.bfloat16)
        copies.append(pltpu.make_async_copy(out_ref.at[rows], out_hbm.at[rows], out_sem.at[r]))
        copies[-1].start()
    for copy in copies:
        copy.wait()


VMEM = pl.BlockSpec(memory_space=pltpu.VMEM)
SMEM = pl.BlockSpec(memory_space=pltpu.SMEM)
HBM = pl.BlockSpec(memory_space=pltpu.HBM)


def call(kernel, out_shapes, in_specs, limit, flops, moved, scratch=(), out_spec=VMEM):
    return pl.pallas_call(
        kernel,
        out_shape=tuple(jax.ShapeDtypeStruct(shape, dtype) for shape, dtype in out_shapes),
        in_specs=in_specs,
        out_specs=tuple(out_spec for _ in out_shapes),
        scratch_shapes=scratch,
        compiler_params=pltpu.CompilerParams(vmem_limit_bytes=limit),
        cost_estimate=pl.CostEstimate(flops=flops, bytes_accessed=moved, transcendentals=0),
    )


def in_hbm(*arrays):
    return tuple(pltpu.with_memory_space_constraint(array, pltpu.HBM) for array in arrays)


def local(ssm_input, gate_input, write_proj, read_proj, decay_codes, decay_rate, skip_gain, norm_gain):
    rows, width = ssm_input.shape
    heads = decay_rate.shape[0]
    blocks = rows // GROUP
    f32, bf16 = jnp.float32, jnp.bfloat16
    (piece,) = call(
        functools.partial(summary_kernel, heads, blocks),
        (((NEAR, PIECE_ROWS, LANES), f32),),
        [HBM] * 4,
        8 * MIB,
        1 << 28,
        3 * MIB,
        (
            pltpu.SMEM(decay_rate.shape, f32),
            pltpu.VMEM(decay_codes.shape, jnp.int32),
            pltpu.VMEM(write_proj.shape, bf16),
            pltpu.VMEM(ssm_input.shape, bf16),
            pltpu.SemaphoreType.DMA((4,)),
        ),
    )(*in_hbm(decay_rate, decay_codes, write_proj, ssm_input))
    got = lax.all_to_all(piece, "near", 0, 0, tiled=True)
    got, later_gate = lax.optimization_barrier((got, gate_input))
    prefix, prefix_decay, total = call(
        near_kernel,
        (((NEAR, STATE, LANES), f32), ((NEAR, PIECE_ROWS - STATE, LANES), f32), ((FAR, PIECE_ROWS, LANES), f32)),
        [VMEM],
        8 * MIB,
        1 << 20,
        MIB,
    )(got)
    totals = lax.all_to_all(total, "far", 0, 0, tiled=True)
    base, factor, lead, own = call(
        functools.partial(inner_kernel, heads, blocks),
        (((rows, width), f32), ((rows, width), f32), ((blocks, width), f32), ((blocks - 1, STATE, width), f32)),
        [HBM] * 7,
        16 * MIB,
        1 << 30,
        7 * MIB,
        (
            pltpu.SMEM(decay_rate.shape, f32),
            pltpu.SMEM(skip_gain.shape, f32),
            pltpu.VMEM(decay_codes.shape, jnp.int32),
            pltpu.VMEM(write_proj.shape, bf16),
            pltpu.VMEM(read_proj.shape, bf16),
            pltpu.VMEM(ssm_input.shape, bf16),
            pltpu.VMEM(gate_input.shape, bf16),
            pltpu.SemaphoreType.DMA((7,)),
        ),
    )(*in_hbm(decay_rate, skip_gain, decay_codes, write_proj, read_proj, ssm_input, later_gate))
    totals, base, factor, lead, own = lax.optimization_barrier((totals, base, factor, lead, own))
    group, row_total = call(
        far_kernel,
        (((PIECE_ROWS, LANES), f32), ((Y, PIECE_ROWS, LANES), f32)),
        [VMEM],
        8 * MIB,
        1 << 33,
        MIB,
    )(totals)
    row_totals = lax.all_to_all(row_total, "y", 0, 0, tiled=True)
    (joint,) = call(join_kernel, (((NEAR, STATE, LANES), f32),), [VMEM] * 4, 8 * MIB, 1 << 33, MIB)(
        row_totals, group, prefix, prefix_decay
    )
    entering = lax.all_to_all(joint, "near", 0, 0, tiled=True)
    gated, power = call(
        functools.partial(carry_kernel, heads, blocks),
        (((rows, width), f32), ((HEAD, rows // LANES, LANES), f32)),
        [VMEM] * 6,
        16 * MIB,
        1 << 28,
        8 * MIB,
    )(entering, own, lead, read_proj, base, factor)
    powers = lax.all_to_all(power, "head", 0, 0, tiled=True)
    (out,) = call(
        functools.partial(norm_kernel, heads),
        (((rows, width), bf16),),
        [VMEM] * 3,
        8 * MIB,
        1 << 20,
        3 * MIB,
        (pltpu.VMEM((rows, width), bf16), pltpu.SemaphoreType.DMA((rows // LANES,))),
        HBM,
    )(powers, norm_gain.reshape(1, width), gated)
    return out


def solution(mesh):
    split = Mesh(mesh.devices.reshape(Y, FAR, NEAR, HEAD), ("y", "far", "near", "head"))
    seq = ("y", "far", "near")
    placed = (
        P(seq, "head"),
        P(seq, "head"),
        P(seq, None),
        P(seq, None),
        P("head", seq),
        P("head"),
        P("head"),
        P("head"),
    )
    return jax.shard_map(local, mesh=split, in_specs=placed, out_specs=P(seq, "head"), check_vma=False)
```

```python
import functools
import math

import jax
import jax.numpy as jnp
from jax import lax
from jax.experimental import pallas as pl
from jax.experimental.pallas import tpu as pltpu
from jax.sharding import Mesh
from jax.sharding import PartitionSpec as P

GROUP = 256
HALF = 128
LANES = 128
CODE_SCALE = 524288.0
CHANNELS = 4096
EPS = 1e-05
Y, FAR, NEAR, HEAD = 4, 4, 4, 8
STATE = 128
OWNERS = Y * NEAR
PIECE = 32
PIECE_ROWS = 40
TOTAL_ROWS = Y * PIECE + 8
MIB = 1 << 20
NT = (((1,), (1,)), ((), ()))
TN = (((0,), (0,)), ((), ()))


def matmul(a, b, dims=(((1,), (0,)), ((), ()))):
    return lax.dot_general(a, b, dims, preferred_element_type=jnp.float32)


def lower_triangle(size):
    row = lax.broadcasted_iota(jnp.int32, (size, size), 0)
    column = lax.broadcasted_iota(jnp.int32, (size, size), 1)
    return row >= column


def code_parts(codes, heads, blocks):
    rows = jnp.concatenate([codes[:, k * GROUP : (k + 1) * GROUP] for k in range(blocks)], axis=0)
    parts = [rows & 255, (rows >> 8) & 255, rows >> 16]
    return jnp.concatenate([part.astype(jnp.float32) for part in parts], axis=0).astype(jnp.bfloat16)


def joined(sums, axis):
    count = sums.shape[axis] // 3
    low, middle, high = (lax.slice_in_dim(sums, i * count, (i + 1) * count, axis=axis) for i in range(3))
    return low + 256.0 * middle + 65536.0 * high


def code_columns(parts, triangle):
    return joined(matmul(triangle, parts, NT), 1)


def code_rows(parts, triangle):
    return joined(matmul(parts, triangle, NT), 0)


def exponent_row(rate_ref, heads, blocks):
    lane = lax.broadcasted_iota(jnp.int32, (1, blocks * heads), 1)
    row = jnp.zeros((1, blocks * heads), jnp.float32)
    for h in range(heads):
        row = jnp.where(lax.rem(lane, heads) == h, rate_ref[h], row)
    return row * (-1.0 / (CODE_SCALE * math.log(2.0)))


def head_lanes(row, start, heads):
    return jnp.concatenate(
        [jnp.broadcast_to(row[:, start + h : start + h + 1], (1, LANES)) for h in range(heads)], axis=1
    )


def weighted_inputs(tail, x_ref, rows, k, heads):
    return jnp.concatenate(
        [
            (tail[:, k * heads + h : k * heads + h + 1] * x_ref[rows, h * LANES : (h + 1) * LANES].astype(jnp.float32))
            .astype(jnp.bfloat16)
            for h in range(heads)
        ],
        axis=1,
    )


def summary_kernel(
    heads,
    blocks,
    rate_hbm,
    codes_hbm,
    write_hbm,
    x_hbm,
    piece_ref,
    rate_ref,
    codes_ref,
    write_ref,
    x_ref,
    sem,
):
    pairs = ((rate_hbm, rate_ref), (codes_hbm, codes_ref), (write_hbm, write_ref), (x_hbm, x_ref))
    copies = [pltpu.make_async_copy(a, b, sem.at[i]) for i, (a, b) in enumerate(pairs)]
    for copy in copies:
        copy.start()
    triangle = lower_triangle(GROUP).astype(jnp.float32).astype(jnp.bfloat16)
    for copy in copies[:2]:
        copy.wait()
    sums = code_columns(code_parts(codes_ref[...], heads, blocks), triangle)
    scale = exponent_row(rate_ref, heads, blocks)
    ends = sums[GROUP - 1 : GROUP, :]
    tail = jnp.exp2((ends - sums) * scale)
    block_decay = jnp.exp2(ends * scale)
    total = sum(ends[:, k * heads : (k + 1) * heads] for k in range(blocks))
    section_decay = jnp.exp2(total * scale[:, :heads])
    for copy in copies[2:]:
        copy.wait()
    state = None
    for k in range(blocks):
        rows = pl.ds(k * GROUP, GROUP)
        added = matmul(write_ref[rows, :], weighted_inputs(tail, x_ref, rows, k, heads), TN)
        state = head_lanes(block_decay, k * heads, heads) * state + added if k else added
    quarters = STATE // PIECE
    for h in range(heads):
        decay = jnp.broadcast_to(section_decay[:, h : h + 1], (PIECE_ROWS - PIECE, LANES))
        for q in range(quarters):
            piece_ref[h * quarters + q, :PIECE, :] = state[q * PIECE : (q + 1) * PIECE, h * LANES : (h + 1) * LANES]
            piece_ref[h * quarters + q, PIECE:, :] = decay


def inner_kernel(
    heads,
    blocks,
    rate_hbm,
    skip_hbm,
    codes_hbm,
    write_hbm,
    read_hbm,
    x_hbm,
    gate_hbm,
    base_ref,
    factor_ref,
    lead_ref,
    local_ref,
    rate_ref,
    skip_ref,
    codes_ref,
    write_ref,
    read_ref,
    x_ref,
    gate_ref,
    sem,
):
    sources = (rate_hbm, skip_hbm, codes_hbm, write_hbm, read_hbm, x_hbm, gate_hbm)
    targets = (rate_ref, skip_ref, codes_ref, write_ref, read_ref, x_ref, gate_ref)
    copies = [pltpu.make_async_copy(a, b, sem.at[i]) for i, (a, b) in enumerate(zip(sources, targets, strict=True))]
    for copy in copies:
        copy.start()
    for copy in copies:
        copy.wait()
    causal = lower_triangle(GROUP)
    triangle = causal.astype(jnp.float32).astype(jnp.bfloat16)
    corner = lower_triangle(HALF)
    parts = code_parts(codes_ref[...], heads, blocks)
    columns = code_columns(parts, triangle)
    across = code_rows(parts, triangle)
    scale = exponent_row(rate_ref, heads, blocks)
    grown = jnp.exp2(columns * scale)
    ends = columns[GROUP - 1 : GROUP, :]
    tail = jnp.exp2((ends - columns) * scale)
    block_decay = jnp.exp2(ends * scale)
    state = None
    for k in range(blocks - 1):
        rows = pl.ds(k * GROUP, GROUP)
        added = matmul(write_ref[rows, :], weighted_inputs(tail, x_ref, rows, k, heads), TN)
        state = head_lanes(block_decay, k * heads, heads) * state + added if k else added
        local_ref[k] = state
    before = jnp.zeros((1, heads), jnp.float32)
    for k in range(blocks):
        lead_ref[k : k + 1, :] = head_lanes(jnp.exp2(before * scale[:, :heads]), 0, heads)
        before = before + ends[:, k * heads : (k + 1) * heads]
    for k in range(blocks):
        rows = pl.ds(k * GROUP, GROUP)
        scores = matmul(read_ref[rows, :], write_ref[rows, :], NT)
        for h in range(heads):
            at = k * heads + h
            lanes = slice(h * LANES, (h + 1) * LANES)
            factor = scale[:, h : h + 1]
            column = columns[:, at : at + 1]
            row = across[at : at + 1, :]

            def mixed(t0, t1, s0, s1, masked):
                decay = jnp.exp2((column[t0:t1] - row[:, s0:s1]) * factor) * scores[t0:t1, s0:s1]
                if masked:
                    decay = jnp.where(corner, decay, 0.0)
                return decay.astype(jnp.bfloat16)

            x_part = x_ref[rows, lanes]
            upper = matmul(mixed(0, HALF, 0, HALF, True), x_part[:HALF])
            lower = jnp.concatenate(
                [mixed(HALF, GROUP, 0, HALF, False), mixed(HALF, GROUP, HALF, GROUP, True)], axis=1
            )
            inner = jnp.concatenate([upper, matmul(lower, x_part)], axis=0)
            gate = gate_ref[rows, lanes].astype(jnp.float32)
            silu = gate / (1.0 + jnp.exp(-gate))
            base_ref[rows, lanes] = (inner + skip_ref[h] * x_part.astype(jnp.float32)) * silu
            factor_ref[rows, lanes] = grown[:, at : at + 1] * silu


def near_kernel(got_ref, prefix_ref, decay_ref, total_ref):
    place = lax.broadcasted_iota(jnp.int32, (TOTAL_ROWS - Y * PIECE, LANES), 0)
    decays = jnp.zeros((TOTAL_ROWS - Y * PIECE, LANES), jnp.float32)
    totals = []
    for y in range(Y):
        state = jnp.zeros((PIECE, LANES), jnp.float32)
        decay = jnp.ones((PIECE_ROWS - PIECE, LANES), jnp.float32)
        for i in range(y * NEAR, (y + 1) * NEAR):
            prefix_ref[i] = state
            decay_ref[i] = decay
            step = got_ref[i, PIECE:, :]
            state = step[:1] * state + got_ref[i, :PIECE, :]
            decay = step * decay
        totals.append(state)
        decays = jnp.where(place == y, decay, decays)
    for j in range(FAR):
        for y in range(Y):
            total_ref[j, y * PIECE : (y + 1) * PIECE, :] = totals[y]
        total_ref[j, Y * PIECE :, :] = decays


def join_kernel(got_ref, prefix_ref, decay_ref, out_ref):
    mine = lax.axis_index("far")
    state = jnp.zeros((PIECE, LANES), jnp.float32)
    for y in range(Y):
        own = state
        for i in range(FAR):
            own = jnp.where(i == mine, state, own)
            decay = got_ref[i, Y * PIECE + y : Y * PIECE + y + 1, :]
            state = decay * state + got_ref[i, y * PIECE : (y + 1) * PIECE, :]
        for i in range(y * NEAR, (y + 1) * NEAR):
            out_ref[i] = decay_ref[i, :1, :] * own + prefix_ref[i]


def carry_kernel(heads, blocks, entering_ref, local_ref, lead_ref, read_ref, base_ref, factor_ref, gated_ref, power_ref):
    quarters = STATE // PIECE
    entering = jnp.concatenate(
        [
            jnp.concatenate([entering_ref[h * quarters + q] for q in range(quarters)], axis=0)
            for h in range(heads)
        ],
        axis=1,
    )
    sums = []
    for k in range(blocks):
        rows = pl.ds(k * GROUP, GROUP)
        state = lead_ref[k : k + 1, :] * entering + local_ref[k - 1] if k else entering
        read_out = matmul(read_ref[rows, :], state.astype(jnp.bfloat16))
        gated = base_ref[rows, :] + factor_ref[rows, :] * read_out
        gated_ref[rows, :] = gated
        squares = gated * gated
        squares = sum(squares[:, h * LANES : (h + 1) * LANES] for h in range(heads))
        for half in range(GROUP // LANES):
            sums.append(jnp.sum(squares[half * LANES : (half + 1) * LANES].T, axis=0, keepdims=True))
    sums = jnp.concatenate(sums, axis=0)
    for j in range(HEAD):
        power_ref[j] = sums


def norm_kernel(heads, power_ref, gain_ref, gated_ref, out_hbm, out_ref, out_sem):
    power = sum(power_ref[j] for j in range(HEAD)) * (1.0 / CHANNELS)
    scale = lax.rsqrt(power + EPS)
    copies = []
    for r in range(scale.shape[0]):
        rows = pl.ds(r * LANES, LANES)
        column = jnp.broadcast_to(scale[r : r + 1, :], (LANES, LANES)).T
        for h in range(heads):
            lanes = slice(h * LANES, (h + 1) * LANES)
            out_ref[rows, lanes] = (gated_ref[rows, lanes] * column * gain_ref[:, lanes]).astype(jnp.bfloat16)
        copies.append(pltpu.make_async_copy(out_ref.at[rows], out_hbm.at[rows], out_sem.at[r]))
        copies[-1].start()
    for copy in copies:
        copy.wait()


VMEM = pl.BlockSpec(memory_space=pltpu.VMEM)
SMEM = pl.BlockSpec(memory_space=pltpu.SMEM)
HBM = pl.BlockSpec(memory_space=pltpu.HBM)


def call(kernel, out_shapes, in_specs, limit, flops, moved, scratch=(), out_spec=VMEM):
    return pl.pallas_call(
        kernel,
        out_shape=tuple(jax.ShapeDtypeStruct(shape, dtype) for shape, dtype in out_shapes),
        in_specs=in_specs,
        out_specs=tuple(out_spec for _ in out_shapes),
        scratch_shapes=scratch,
        compiler_params=pltpu.CompilerParams(vmem_limit_bytes=limit),
        cost_estimate=pl.CostEstimate(flops=flops, bytes_accessed=moved, transcendentals=0),
    )


def in_hbm(*arrays):
    return tuple(pltpu.with_memory_space_constraint(array, pltpu.HBM) for array in arrays)


def local(ssm_input, gate_input, write_proj, read_proj, decay_codes, decay_rate, skip_gain, norm_gain):
    rows, width = ssm_input.shape
    heads = decay_rate.shape[0]
    blocks = rows // GROUP
    f32, bf16 = jnp.float32, jnp.bfloat16
    (piece,) = call(
        functools.partial(summary_kernel, heads, blocks),
        (((OWNERS, PIECE_ROWS, LANES), f32),),
        [HBM] * 4,
        8 * MIB,
        1 << 28,
        3 * MIB,
        (
            pltpu.SMEM(decay_rate.shape, f32),
            pltpu.VMEM(decay_codes.shape, jnp.int32),
            pltpu.VMEM(write_proj.shape, bf16),
            pltpu.VMEM(ssm_input.shape, bf16),
            pltpu.SemaphoreType.DMA((4,)),
        ),
    )(*in_hbm(decay_rate, decay_codes, write_proj, ssm_input))
    got = lax.all_to_all(piece, ("y", "near"), 0, 0, tiled=True)
    got, later_gate = lax.optimization_barrier((got, gate_input))
    prefix, prefix_decay, total = call(
        near_kernel,
        (((OWNERS, PIECE, LANES), f32), ((OWNERS, PIECE_ROWS - PIECE, LANES), f32), ((FAR, TOTAL_ROWS, LANES), f32)),
        [VMEM],
        8 * MIB,
        1 << 20,
        MIB,
    )(got)
    totals = lax.all_to_all(total, "far", 0, 0, tiled=True)
    base, factor, lead, own = call(
        functools.partial(inner_kernel, heads, blocks),
        (((rows, width), f32), ((rows, width), f32), ((blocks, width), f32), ((blocks - 1, STATE, width), f32)),
        [HBM] * 7,
        16 * MIB,
        1 << 30,
        7 * MIB,
        (
            pltpu.SMEM(decay_rate.shape, f32),
            pltpu.SMEM(skip_gain.shape, f32),
            pltpu.VMEM(decay_codes.shape, jnp.int32),
            pltpu.VMEM(write_proj.shape, bf16),
            pltpu.VMEM(read_proj.shape, bf16),
            pltpu.VMEM(ssm_input.shape, bf16),
            pltpu.VMEM(gate_input.shape, bf16),
            pltpu.SemaphoreType.DMA((7,)),
        ),
    )(*in_hbm(decay_rate, skip_gain, decay_codes, write_proj, read_proj, ssm_input, later_gate))
    totals, base, factor, lead, own = lax.optimization_barrier((totals, base, factor, lead, own))
    (joint,) = call(join_kernel, (((OWNERS, PIECE, LANES), f32),), [VMEM] * 3, 8 * MIB, 1 << 33, MIB)(
        totals, prefix, prefix_decay
    )
    entering = lax.all_to_all(joint, ("y", "near"), 0, 0, tiled=True)
    gated, power = call(
        functools.partial(carry_kernel, heads, blocks),
        (((rows, width), f32), ((HEAD, rows // LANES, LANES), f32)),
        [VMEM] * 6,
        16 * MIB,
        1 << 28,
        8 * MIB,
    )(entering, own, lead, read_proj, base, factor)
    powers = lax.all_to_all(power, "head", 0, 0, tiled=True)
    (out,) = call(
        functools.partial(norm_kernel, heads),
        (((rows, width), bf16),),
        [VMEM] * 3,
        8 * MIB,
        1 << 20,
        3 * MIB,
        (pltpu.VMEM((rows, width), bf16), pltpu.SemaphoreType.DMA((rows // LANES,))),
        HBM,
    )(powers, norm_gain.reshape(1, width), gated)
    return out


def solution(mesh):
    split = Mesh(mesh.devices.reshape(Y, FAR, NEAR, HEAD), ("y", "far", "near", "head"))
    seq = ("y", "far", "near")
    placed = (
        P(seq, "head"),
        P(seq, "head"),
        P(seq, None),
        P(seq, None),
        P("head", seq),
        P("head"),
        P("head"),
        P("head"),
    )
    return jax.shard_map(local, mesh=split, in_specs=placed, out_specs=P(seq, "head"), check_vma=False)
```

```python
import functools
import math

import jax
import jax.numpy as jnp
from jax import lax
from jax.experimental import pallas as pl
from jax.experimental.pallas import tpu as pltpu
from jax.sharding import Mesh
from jax.sharding import PartitionSpec as P

GROUP = 256
HALF = 128
LANES = 128
CODE_SCALE = 524288.0
CHANNELS = 4096
EPS = 1e-05
Y, FAR, NEAR, HEAD = 4, 4, 4, 8
STATE = 128
OWNERS = Y * NEAR
PIECE = 32
PIECE_ROWS = 40
TOTAL_ROWS = Y * PIECE + 8
MIB = 1 << 20
NT = (((1,), (1,)), ((), ()))
TN = (((0,), (0,)), ((), ()))


def matmul(a, b, dims=(((1,), (0,)), ((), ()))):
    return lax.dot_general(a, b, dims, preferred_element_type=jnp.float32)


def lower_triangle(size):
    row = lax.broadcasted_iota(jnp.int32, (size, size), 0)
    column = lax.broadcasted_iota(jnp.int32, (size, size), 1)
    return row >= column


def code_parts(codes, heads, blocks):
    rows = jnp.concatenate([codes[:, k * GROUP : (k + 1) * GROUP] for k in range(blocks)], axis=0)
    parts = [rows & 255, (rows >> 8) & 255, rows >> 16]
    return jnp.concatenate([part.astype(jnp.float32) for part in parts], axis=0).astype(jnp.bfloat16)


def joined(sums, axis):
    count = sums.shape[axis] // 3
    low, middle, high = (lax.slice_in_dim(sums, i * count, (i + 1) * count, axis=axis) for i in range(3))
    return low + 256.0 * middle + 65536.0 * high


def code_columns(parts, triangle):
    return joined(matmul(triangle, parts, NT), 1)


def code_rows(parts, triangle):
    return joined(matmul(parts, triangle, NT), 0)


def exponent_row(rate_ref, heads, blocks):
    lane = lax.broadcasted_iota(jnp.int32, (1, blocks * heads), 1)
    row = jnp.zeros((1, blocks * heads), jnp.float32)
    for h in range(heads):
        row = jnp.where(lax.rem(lane, heads) == h, rate_ref[h], row)
    return row * (-1.0 / (CODE_SCALE * math.log(2.0)))


def head_lanes(row, start, heads):
    return jnp.concatenate(
        [jnp.broadcast_to(row[:, start + h : start + h + 1], (1, LANES)) for h in range(heads)], axis=1
    )


def weighted_inputs(tail, x_ref, rows, k, heads):
    return jnp.concatenate(
        [
            (tail[:, k * heads + h : k * heads + h + 1] * x_ref[rows, h * LANES : (h + 1) * LANES].astype(jnp.float32))
            .astype(jnp.bfloat16)
            for h in range(heads)
        ],
        axis=1,
    )


def summary_kernel(
    heads,
    blocks,
    rate_hbm,
    codes_hbm,
    write_hbm,
    x_hbm,
    piece_ref,
    rate_ref,
    codes_ref,
    write_ref,
    x_ref,
    sem,
):
    pairs = ((rate_hbm, rate_ref), (codes_hbm, codes_ref), (write_hbm, write_ref), (x_hbm, x_ref))
    copies = [pltpu.make_async_copy(a, b, sem.at[i]) for i, (a, b) in enumerate(pairs)]
    for copy in copies:
        copy.start()
    triangle = lower_triangle(GROUP).astype(jnp.float32).astype(jnp.bfloat16)
    for copy in copies[:2]:
        copy.wait()
    sums = code_columns(code_parts(codes_ref[...], heads, blocks), triangle)
    scale = exponent_row(rate_ref, heads, blocks)
    ends = sums[GROUP - 1 : GROUP, :]
    tail = jnp.exp2((ends - sums) * scale)
    block_decay = jnp.exp2(ends * scale)
    total = sum(ends[:, k * heads : (k + 1) * heads] for k in range(blocks))
    section_decay = jnp.exp2(total * scale[:, :heads])
    for copy in copies[2:]:
        copy.wait()
    state = None
    for k in range(blocks):
        rows = pl.ds(k * GROUP, GROUP)
        added = matmul(write_ref[rows, :], weighted_inputs(tail, x_ref, rows, k, heads), TN)
        state = head_lanes(block_decay, k * heads, heads) * state + added if k else added
    quarters = STATE // PIECE
    for h in range(heads):
        decay = jnp.broadcast_to(section_decay[:, h : h + 1], (PIECE_ROWS - PIECE, LANES))
        for q in range(quarters):
            piece_ref[h * quarters + q, :PIECE, :] = state[q * PIECE : (q + 1) * PIECE, h * LANES : (h + 1) * LANES]
            piece_ref[h * quarters + q, PIECE:, :] = decay


def inner_kernel(
    heads,
    blocks,
    rate_hbm,
    skip_hbm,
    codes_hbm,
    write_hbm,
    read_hbm,
    x_hbm,
    gate_hbm,
    base_ref,
    factor_ref,
    lead_ref,
    local_ref,
    rate_ref,
    skip_ref,
    codes_ref,
    write_ref,
    read_ref,
    x_ref,
    gate_ref,
    sem,
):
    sources = (rate_hbm, skip_hbm, codes_hbm, write_hbm, read_hbm, x_hbm, gate_hbm)
    targets = (rate_ref, skip_ref, codes_ref, write_ref, read_ref, x_ref, gate_ref)
    copies = [pltpu.make_async_copy(a, b, sem.at[i]) for i, (a, b) in enumerate(zip(sources, targets, strict=True))]
    for copy in copies:
        copy.start()
    for copy in copies:
        copy.wait()
    causal = lower_triangle(GROUP)
    triangle = causal.astype(jnp.float32).astype(jnp.bfloat16)
    corner = lower_triangle(HALF)
    parts = code_parts(codes_ref[...], heads, blocks)
    columns = code_columns(parts, triangle)
    across = code_rows(parts, triangle)
    scale = exponent_row(rate_ref, heads, blocks)
    grown = jnp.exp2(columns * scale)
    ends = columns[GROUP - 1 : GROUP, :]
    tail = jnp.exp2((ends - columns) * scale)
    block_decay = jnp.exp2(ends * scale)
    state = None
    for k in range(blocks - 1):
        rows = pl.ds(k * GROUP, GROUP)
        added = matmul(write_ref[rows, :], weighted_inputs(tail, x_ref, rows, k, heads), TN)
        state = head_lanes(block_decay, k * heads, heads) * state + added if k else added
        local_ref[k] = state
    before = jnp.zeros((1, heads), jnp.float32)
    for k in range(blocks):
        lead_ref[k : k + 1, :] = head_lanes(jnp.exp2(before * scale[:, :heads]), 0, heads)
        before = before + ends[:, k * heads : (k + 1) * heads]
    for k in range(blocks):
        rows = pl.ds(k * GROUP, GROUP)
        scores = matmul(read_ref[rows, :], write_ref[rows, :], NT)
        for h in range(heads):
            at = k * heads + h
            lanes = slice(h * LANES, (h + 1) * LANES)
            factor = scale[:, h : h + 1]
            column = columns[:, at : at + 1]
            row = across[at : at + 1, :]

            def mixed(t0, t1, s0, s1, masked):
                decay = jnp.exp2((column[t0:t1] - row[:, s0:s1]) * factor) * scores[t0:t1, s0:s1]
                if masked:
                    decay = jnp.where(corner, decay, 0.0)
                return decay.astype(jnp.bfloat16)

            x_part = x_ref[rows, lanes]
            upper = matmul(mixed(0, HALF, 0, HALF, True), x_part[:HALF])
            lower = jnp.concatenate(
                [mixed(HALF, GROUP, 0, HALF, False), mixed(HALF, GROUP, HALF, GROUP, True)], axis=1
            )
            inner = jnp.concatenate([upper, matmul(lower, x_part)], axis=0)
            gate = gate_ref[rows, lanes].astype(jnp.float32)
            silu = gate / (1.0 + jnp.exp(-gate))
            base_ref[rows, lanes] = (inner + skip_ref[h] * x_part.astype(jnp.float32)) * silu
            factor_ref[rows, lanes] = grown[:, at : at + 1] * silu


def near_kernel(got_ref, prefix_ref, decay_ref, total_ref):
    place = lax.broadcasted_iota(jnp.int32, (TOTAL_ROWS - Y * PIECE, LANES), 0)
    decays = jnp.zeros((TOTAL_ROWS - Y * PIECE, LANES), jnp.float32)
    totals = []
    for y in range(Y):
        state = jnp.zeros((PIECE, LANES), jnp.float32)
        decay = jnp.ones((PIECE_ROWS - PIECE, LANES), jnp.float32)
        for i in range(y * NEAR, (y + 1) * NEAR):
            prefix_ref[i] = state
            decay_ref[i] = decay
            step = got_ref[i, PIECE:, :]
            state = step[:1] * state + got_ref[i, :PIECE, :]
            decay = step * decay
        totals.append(state)
        decays = jnp.where(place == y, decay, decays)
    for y in range(Y):
        total_ref[y * PIECE : (y + 1) * PIECE, :] = totals[y]
    total_ref[Y * PIECE :, :] = decays


def join_kernel(got_ref, prefix_ref, decay_ref, out_ref):
    mine = lax.axis_index("far")
    state = jnp.zeros((PIECE, LANES), jnp.float32)
    for y in range(Y):
        own = state
        for i in range(FAR):
            own = jnp.where(i == mine, state, own)
            decay = got_ref[i, Y * PIECE + y : Y * PIECE + y + 1, :]
            state = decay * state + got_ref[i, y * PIECE : (y + 1) * PIECE, :]
        for i in range(y * NEAR, (y + 1) * NEAR):
            out_ref[i] = decay_ref[i, :1, :] * own + prefix_ref[i]


def carry_kernel(heads, blocks, entering_ref, local_ref, lead_ref, read_ref, base_ref, factor_ref, gated_ref, power_ref):
    quarters = STATE // PIECE
    entering = jnp.concatenate(
        [
            jnp.concatenate([entering_ref[h * quarters + q] for q in range(quarters)], axis=0)
            for h in range(heads)
        ],
        axis=1,
    )
    sums = []
    for k in range(blocks):
        rows = pl.ds(k * GROUP, GROUP)
        state = lead_ref[k : k + 1, :] * entering + local_ref[k - 1] if k else entering
        read_out = matmul(read_ref[rows, :], state.astype(jnp.bfloat16))
        gated = base_ref[rows, :] + factor_ref[rows, :] * read_out
        gated_ref[rows, :] = gated
        squares = gated * gated
        squares = sum(squares[:, h * LANES : (h + 1) * LANES] for h in range(heads))
        for half in range(GROUP // LANES):
            sums.append(jnp.sum(squares[half * LANES : (half + 1) * LANES].T, axis=0, keepdims=True))
    sums = jnp.concatenate(sums, axis=0)
    for j in range(HEAD):
        power_ref[j] = sums


def norm_kernel(heads, power_ref, gain_ref, gated_ref, out_hbm, out_ref, out_sem):
    power = sum(power_ref[j] for j in range(HEAD)) * (1.0 / CHANNELS)
    scale = lax.rsqrt(power + EPS)
    copies = []
    for r in range(scale.shape[0]):
        rows = pl.ds(r * LANES, LANES)
        column = jnp.broadcast_to(scale[r : r + 1, :], (LANES, LANES)).T
        for h in range(heads):
            lanes = slice(h * LANES, (h + 1) * LANES)
            out_ref[rows, lanes] = (gated_ref[rows, lanes] * column * gain_ref[:, lanes]).astype(jnp.bfloat16)
        copies.append(pltpu.make_async_copy(out_ref.at[rows], out_hbm.at[rows], out_sem.at[r]))
        copies[-1].start()
    for copy in copies:
        copy.wait()


VMEM = pl.BlockSpec(memory_space=pltpu.VMEM)
SMEM = pl.BlockSpec(memory_space=pltpu.SMEM)
HBM = pl.BlockSpec(memory_space=pltpu.HBM)


def call(kernel, out_shapes, in_specs, limit, flops, moved, scratch=(), out_spec=VMEM):
    return pl.pallas_call(
        kernel,
        out_shape=tuple(jax.ShapeDtypeStruct(shape, dtype) for shape, dtype in out_shapes),
        in_specs=in_specs,
        out_specs=tuple(out_spec for _ in out_shapes),
        scratch_shapes=scratch,
        compiler_params=pltpu.CompilerParams(vmem_limit_bytes=limit),
        cost_estimate=pl.CostEstimate(flops=flops, bytes_accessed=moved, transcendentals=0),
    )


def in_hbm(*arrays):
    return tuple(pltpu.with_memory_space_constraint(array, pltpu.HBM) for array in arrays)


def local(ssm_input, gate_input, write_proj, read_proj, decay_codes, decay_rate, skip_gain, norm_gain):
    rows, width = ssm_input.shape
    heads = decay_rate.shape[0]
    blocks = rows // GROUP
    f32, bf16 = jnp.float32, jnp.bfloat16
    (piece,) = call(
        functools.partial(summary_kernel, heads, blocks),
        (((OWNERS, PIECE_ROWS, LANES), f32),),
        [HBM] * 4,
        8 * MIB,
        1 << 28,
        3 * MIB,
        (
            pltpu.SMEM(decay_rate.shape, f32),
            pltpu.VMEM(decay_codes.shape, jnp.int32),
            pltpu.VMEM(write_proj.shape, bf16),
            pltpu.VMEM(ssm_input.shape, bf16),
            pltpu.SemaphoreType.DMA((4,)),
        ),
    )(*in_hbm(decay_rate, decay_codes, write_proj, ssm_input))
    got = lax.all_to_all(piece, ("y", "near"), 0, 0, tiled=True)
    base, factor, lead, own = call(
        functools.partial(inner_kernel, heads, blocks),
        (((rows, width), f32), ((rows, width), f32), ((blocks, width), f32), ((blocks - 1, STATE, width), f32)),
        [HBM] * 7,
        16 * MIB,
        1 << 30,
        7 * MIB,
        (
            pltpu.SMEM(decay_rate.shape, f32),
            pltpu.SMEM(skip_gain.shape, f32),
            pltpu.VMEM(decay_codes.shape, jnp.int32),
            pltpu.VMEM(write_proj.shape, bf16),
            pltpu.VMEM(read_proj.shape, bf16),
            pltpu.VMEM(ssm_input.shape, bf16),
            pltpu.VMEM(gate_input.shape, bf16),
            pltpu.SemaphoreType.DMA((7,)),
        ),
    )(*in_hbm(decay_rate, skip_gain, decay_codes, write_proj, read_proj, ssm_input, gate_input))
    got, base, factor, lead, own = lax.optimization_barrier((got, base, factor, lead, own))
    prefix, prefix_decay, total = call(
        near_kernel,
        (((OWNERS, PIECE, LANES), f32), ((OWNERS, PIECE_ROWS - PIECE, LANES), f32), ((TOTAL_ROWS, LANES), f32)),
        [VMEM],
        8 * MIB,
        1 << 33,
        MIB,
    )(got)
    totals = lax.all_gather(total, "far")
    (joint,) = call(join_kernel, (((OWNERS, PIECE, LANES), f32),), [VMEM] * 3, 8 * MIB, 1 << 33, MIB)(
        totals, prefix, prefix_decay
    )
    entering = lax.all_to_all(joint, ("y", "near"), 0, 0, tiled=True)
    gated, power = call(
        functools.partial(carry_kernel, heads, blocks),
        (((rows, width), f32), ((HEAD, rows // LANES, LANES), f32)),
        [VMEM] * 6,
        16 * MIB,
        1 << 28,
        8 * MIB,
    )(entering, own, lead, read_proj, base, factor)
    powers = lax.all_to_all(power, "head", 0, 0, tiled=True)
    (out,) = call(
        functools.partial(norm_kernel, heads),
        (((rows, width), bf16),),
        [VMEM] * 3,
        8 * MIB,
        1 << 20,
        3 * MIB,
        (pltpu.VMEM((rows, width), bf16), pltpu.SemaphoreType.DMA((rows // LANES,))),
        HBM,
    )(powers, norm_gain.reshape(1, width), gated)
    return out


def solution(mesh):
    split = Mesh(mesh.devices.reshape(Y, FAR, NEAR, HEAD), ("y", "far", "near", "head"))
    seq = ("y", "far", "near")
    placed = (
        P(seq, "head"),
        P(seq, "head"),
        P(seq, None),
        P(seq, None),
        P("head", seq),
        P("head"),
        P("head"),
        P("head"),
    )
    return jax.shard_map(local, mesh=split, in_specs=placed, out_specs=P(seq, "head"), check_vma=False)
```

```python
import functools
import math

import jax
import jax.numpy as jnp
from jax import lax
from jax.experimental import pallas as pl
from jax.experimental.pallas import tpu as pltpu
from jax.sharding import Mesh
from jax.sharding import PartitionSpec as P

GROUP = 256
HALF = 128
LANES = 128
CODE_SCALE = 524288.0
CHANNELS = 4096
EPS = 1e-05
Y, FAR, NEAR, HEAD = 4, 4, 4, 8
STATE = 128
OWNERS = Y * NEAR
PIECE = 32
PIECE_ROWS = 40
TOTAL_ROWS = Y * PIECE + 8
MIB = 1 << 20
NT = (((1,), (1,)), ((), ()))
TN = (((0,), (0,)), ((), ()))


def matmul(a, b, dims=(((1,), (0,)), ((), ()))):
    return lax.dot_general(a, b, dims, preferred_element_type=jnp.float32)


def lower_triangle(size):
    row = lax.broadcasted_iota(jnp.int32, (size, size), 0)
    column = lax.broadcasted_iota(jnp.int32, (size, size), 1)
    return row >= column


def code_parts(codes, heads, blocks):
    rows = jnp.concatenate([codes[:, k * GROUP : (k + 1) * GROUP] for k in range(blocks)], axis=0)
    parts = [rows & 255, (rows >> 8) & 255, rows >> 16]
    return jnp.concatenate([part.astype(jnp.float32) for part in parts], axis=0).astype(jnp.bfloat16)


def joined(sums, axis):
    count = sums.shape[axis] // 3
    low, middle, high = (lax.slice_in_dim(sums, i * count, (i + 1) * count, axis=axis) for i in range(3))
    return low + 256.0 * middle + 65536.0 * high


def code_columns(parts, triangle):
    return joined(matmul(triangle, parts, NT), 1)


def code_rows(parts, triangle):
    return joined(matmul(parts, triangle, NT), 0)


def exponent_row(rate_ref, heads, blocks):
    lane = lax.broadcasted_iota(jnp.int32, (1, blocks * heads), 1)
    row = jnp.zeros((1, blocks * heads), jnp.float32)
    for h in range(heads):
        row = jnp.where(lax.rem(lane, heads) == h, rate_ref[h], row)
    return row * (-1.0 / (CODE_SCALE * math.log(2.0)))


def head_lanes(row, start, heads):
    return jnp.concatenate(
        [jnp.broadcast_to(row[:, start + h : start + h + 1], (1, LANES)) for h in range(heads)], axis=1
    )


def weighted_inputs(tail, x_ref, rows, k, heads):
    return jnp.concatenate(
        [
            (tail[:, k * heads + h : k * heads + h + 1] * x_ref[rows, h * LANES : (h + 1) * LANES].astype(jnp.float32))
            .astype(jnp.bfloat16)
            for h in range(heads)
        ],
        axis=1,
    )


def summary_kernel(
    heads,
    blocks,
    rate_hbm,
    codes_hbm,
    write_hbm,
    x_hbm,
    piece_hbm,
    rate_ref,
    codes_ref,
    write_ref,
    x_ref,
    piece_ref,
    sem,
    out_sem,
):
    pairs = ((rate_hbm, rate_ref), (codes_hbm, codes_ref), (x_hbm, x_ref), (write_hbm, write_ref))
    copies = [pltpu.make_async_copy(a, b, sem.at[i]) for i, (a, b) in enumerate(pairs)]
    for copy in copies:
        copy.start()
    triangle = lower_triangle(GROUP).astype(jnp.float32).astype(jnp.bfloat16)
    for copy in copies[:2]:
        copy.wait()
    sums = code_columns(code_parts(codes_ref[...], heads, blocks), triangle)
    scale = exponent_row(rate_ref, heads, blocks)
    ends = sums[GROUP - 1 : GROUP, :]
    tail = jnp.exp2((ends - sums) * scale)
    block_decay = jnp.exp2(ends * scale)
    total = sum(ends[:, k * heads : (k + 1) * heads] for k in range(blocks))
    section_decay = jnp.exp2(total * scale[:, :heads])
    for copy in copies[2:]:
        copy.wait()
    state = None
    for k in range(blocks):
        rows = pl.ds(k * GROUP, GROUP)
        added = matmul(write_ref[rows, :], weighted_inputs(tail, x_ref, rows, k, heads), TN)
        state = head_lanes(block_decay, k * heads, heads) * state + added if k else added
    quarters = STATE // PIECE
    sent = []
    for h in range(heads):
        decay = jnp.broadcast_to(section_decay[:, h : h + 1], (PIECE_ROWS - PIECE, LANES))
        for q in range(quarters):
            piece_ref[h * quarters + q, :PIECE, :] = state[q * PIECE : (q + 1) * PIECE, h * LANES : (h + 1) * LANES]
            piece_ref[h * quarters + q, PIECE:, :] = decay
        own = pl.ds(h * quarters, quarters)
        sent.append(pltpu.make_async_copy(piece_ref.at[own], piece_hbm.at[own], out_sem.at[h]))
        sent[-1].start()
    for copy in sent:
        copy.wait()


def inner_kernel(
    heads,
    blocks,
    rate_hbm,
    skip_hbm,
    codes_hbm,
    write_hbm,
    read_hbm,
    x_hbm,
    gate_hbm,
    base_ref,
    factor_ref,
    lead_ref,
    local_ref,
    rate_ref,
    skip_ref,
    codes_ref,
    write_ref,
    read_ref,
    x_ref,
    gate_ref,
    sem,
):
    sources = (rate_hbm, skip_hbm, codes_hbm, write_hbm, read_hbm, x_hbm, gate_hbm)
    targets = (rate_ref, skip_ref, codes_ref, write_ref, read_ref, x_ref, gate_ref)
    copies = [pltpu.make_async_copy(a, b, sem.at[i]) for i, (a, b) in enumerate(zip(sources, targets, strict=True))]
    for copy in copies:
        copy.start()
    for copy in copies:
        copy.wait()
    causal = lower_triangle(GROUP)
    triangle = causal.astype(jnp.float32).astype(jnp.bfloat16)
    corner = lower_triangle(HALF)
    parts = code_parts(codes_ref[...], heads, blocks)
    columns = code_columns(parts, triangle)
    across = code_rows(parts, triangle)
    scale = exponent_row(rate_ref, heads, blocks)
    grown = jnp.exp2(columns * scale)
    ends = columns[GROUP - 1 : GROUP, :]
    tail = jnp.exp2((ends - columns) * scale)
    block_decay = jnp.exp2(ends * scale)
    state = None
    for k in range(blocks - 1):
        rows = pl.ds(k * GROUP, GROUP)
        added = matmul(write_ref[rows, :], weighted_inputs(tail, x_ref, rows, k, heads), TN)
        state = head_lanes(block_decay, k * heads, heads) * state + added if k else added
        local_ref[k] = state
    before = jnp.zeros((1, heads), jnp.float32)
    for k in range(blocks):
        lead_ref[k : k + 1, :] = head_lanes(jnp.exp2(before * scale[:, :heads]), 0, heads)
        before = before + ends[:, k * heads : (k + 1) * heads]
    for k in range(blocks):
        rows = pl.ds(k * GROUP, GROUP)
        scores = matmul(read_ref[rows, :], write_ref[rows, :], NT)
        for h in range(heads):
            at = k * heads + h
            lanes = slice(h * LANES, (h + 1) * LANES)
            factor = scale[:, h : h + 1]
            column = columns[:, at : at + 1]
            row = across[at : at + 1, :]

            def mixed(t0, t1, s0, s1, masked):
                decay = jnp.exp2((column[t0:t1] - row[:, s0:s1]) * factor) * scores[t0:t1, s0:s1]
                if masked:
                    decay = jnp.where(corner, decay, 0.0)
                return decay.astype(jnp.bfloat16)

            x_part = x_ref[rows, lanes]
            upper = matmul(mixed(0, HALF, 0, HALF, True), x_part[:HALF])
            lower = jnp.concatenate(
                [mixed(HALF, GROUP, 0, HALF, False), mixed(HALF, GROUP, HALF, GROUP, True)], axis=1
            )
            inner = jnp.concatenate([upper, matmul(lower, x_part)], axis=0)
            gate = gate_ref[rows, lanes].astype(jnp.float32)
            silu = gate / (1.0 + jnp.exp(-gate))
            base_ref[rows, lanes] = (inner + skip_ref[h] * x_part.astype(jnp.float32)) * silu
            factor_ref[rows, lanes] = grown[:, at : at + 1] * silu


def near_kernel(got_ref, prefix_ref, decay_ref, total_ref):
    place = lax.broadcasted_iota(jnp.int32, (TOTAL_ROWS - Y * PIECE, LANES), 0)
    decays = jnp.zeros((TOTAL_ROWS - Y * PIECE, LANES), jnp.float32)
    totals = []
    for y in range(Y):
        state = jnp.zeros((PIECE, LANES), jnp.float32)
        decay = jnp.ones((PIECE_ROWS - PIECE, LANES), jnp.float32)
        for i in range(y * NEAR, (y + 1) * NEAR):
            prefix_ref[i] = state
            decay_ref[i] = decay
            step = got_ref[i, PIECE:, :]
            state = step[:1] * state + got_ref[i, :PIECE, :]
            decay = step * decay
        totals.append(state)
        decays = jnp.where(place == y, decay, decays)
    for y in range(Y):
        total_ref[y * PIECE : (y + 1) * PIECE, :] = totals[y]
    total_ref[Y * PIECE :, :] = decays


def join_kernel(got_ref, prefix_ref, decay_ref, out_ref):
    mine = lax.axis_index("far")
    state = jnp.zeros((PIECE, LANES), jnp.float32)
    for y in range(Y):
        own = state
        for i in range(FAR):
            own = jnp.where(i == mine, state, own)
            decay = got_ref[i, Y * PIECE + y : Y * PIECE + y + 1, :]
            state = decay * state + got_ref[i, y * PIECE : (y + 1) * PIECE, :]
        for i in range(y * NEAR, (y + 1) * NEAR):
            out_ref[i] = decay_ref[i, :1, :] * own + prefix_ref[i]


def carry_kernel(heads, blocks, entering_ref, local_ref, lead_ref, read_ref, base_ref, factor_ref, gated_ref, power_ref):
    quarters = STATE // PIECE
    entering = jnp.concatenate(
        [
            jnp.concatenate([entering_ref[h * quarters + q] for q in range(quarters)], axis=0)
            for h in range(heads)
        ],
        axis=1,
    )
    sums = []
    for k in range(blocks):
        rows = pl.ds(k * GROUP, GROUP)
        state = lead_ref[k : k + 1, :] * entering + local_ref[k - 1] if k else entering
        read_out = matmul(read_ref[rows, :], state.astype(jnp.bfloat16))
        gated = base_ref[rows, :] + factor_ref[rows, :] * read_out
        gated_ref[rows, :] = gated
        squares = gated * gated
        squares = sum(squares[:, h * LANES : (h + 1) * LANES] for h in range(heads))
        for half in range(GROUP // LANES):
            sums.append(jnp.sum(squares[half * LANES : (half + 1) * LANES].T, axis=0, keepdims=True))
    sums = jnp.concatenate(sums, axis=0)
    for j in range(HEAD):
        power_ref[j] = sums


def norm_kernel(heads, power_ref, gain_ref, gated_ref, out_hbm, out_ref, out_sem):
    power = sum(power_ref[j] for j in range(HEAD)) * (1.0 / CHANNELS)
    scale = lax.rsqrt(power + EPS)
    columns = [jnp.broadcast_to(scale[r : r + 1, :], (LANES, LANES)).T for r in range(scale.shape[0])]
    copies = []
    for r in range(scale.shape[0]):
        rows = pl.ds(r * LANES, LANES)
        column = columns[r]
        for h in range(heads):
            lanes = slice(h * LANES, (h + 1) * LANES)
            out_ref[rows, lanes] = (gated_ref[rows, lanes] * column * gain_ref[:, lanes]).astype(jnp.bfloat16)
        copies.append(pltpu.make_async_copy(out_ref.at[rows], out_hbm.at[rows], out_sem.at[r]))
        copies[-1].start()
    for copy in copies:
        copy.wait()


VMEM = pl.BlockSpec(memory_space=pltpu.VMEM)
SMEM = pl.BlockSpec(memory_space=pltpu.SMEM)
HBM = pl.BlockSpec(memory_space=pltpu.HBM)


def call(kernel, out_shapes, in_specs, limit, flops, moved, scratch=(), out_spec=VMEM):
    return pl.pallas_call(
        kernel,
        out_shape=tuple(jax.ShapeDtypeStruct(shape, dtype) for shape, dtype in out_shapes),
        in_specs=in_specs,
        out_specs=tuple(out_spec for _ in out_shapes),
        scratch_shapes=scratch,
        compiler_params=pltpu.CompilerParams(vmem_limit_bytes=limit),
        cost_estimate=pl.CostEstimate(flops=flops, bytes_accessed=moved, transcendentals=0),
    )


def in_hbm(*arrays):
    return tuple(pltpu.with_memory_space_constraint(array, pltpu.HBM) for array in arrays)


def local(ssm_input, gate_input, write_proj, read_proj, decay_codes, decay_rate, skip_gain, norm_gain):
    rows, width = ssm_input.shape
    heads = decay_rate.shape[0]
    blocks = rows // GROUP
    f32, bf16 = jnp.float32, jnp.bfloat16
    (piece,) = call(
        functools.partial(summary_kernel, heads, blocks),
        (((OWNERS, PIECE_ROWS, LANES), f32),),
        [HBM] * 4,
        8 * MIB,
        1 << 28,
        3 * MIB,
        (
            pltpu.SMEM(decay_rate.shape, f32),
            pltpu.VMEM(decay_codes.shape, jnp.int32),
            pltpu.VMEM(write_proj.shape, bf16),
            pltpu.VMEM(ssm_input.shape, bf16),
            pltpu.VMEM((OWNERS, PIECE_ROWS, LANES), f32),
            pltpu.SemaphoreType.DMA((4,)),
            pltpu.SemaphoreType.DMA((heads,)),
        ),
        HBM,
    )(*in_hbm(decay_rate, decay_codes, write_proj, ssm_input))
    got = lax.all_to_all(piece, ("y", "near"), 0, 0, tiled=True)
    base, factor, lead, own = call(
        functools.partial(inner_kernel, heads, blocks),
        (((rows, width), f32), ((rows, width), f32), ((blocks, width), f32), ((blocks - 1, STATE, width), f32)),
        [HBM] * 7,
        16 * MIB,
        1 << 30,
        7 * MIB,
        (
            pltpu.SMEM(decay_rate.shape, f32),
            pltpu.SMEM(skip_gain.shape, f32),
            pltpu.VMEM(decay_codes.shape, jnp.int32),
            pltpu.VMEM(write_proj.shape, bf16),
            pltpu.VMEM(read_proj.shape, bf16),
            pltpu.VMEM(ssm_input.shape, bf16),
            pltpu.VMEM(gate_input.shape, bf16),
            pltpu.SemaphoreType.DMA((7,)),
        ),
    )(*in_hbm(decay_rate, skip_gain, decay_codes, write_proj, read_proj, ssm_input, gate_input))
    got, base, factor, lead, own = lax.optimization_barrier((got, base, factor, lead, own))
    prefix, prefix_decay, total = call(
        near_kernel,
        (((OWNERS, PIECE, LANES), f32), ((OWNERS, PIECE_ROWS - PIECE, LANES), f32), ((TOTAL_ROWS, LANES), f32)),
        [VMEM],
        8 * MIB,
        1 << 33,
        MIB,
    )(got)
    totals = lax.all_gather(total, "far")
    (joint,) = call(join_kernel, (((OWNERS, PIECE, LANES), f32),), [VMEM] * 3, 8 * MIB, 1 << 33, MIB)(
        totals, prefix, prefix_decay
    )
    entering = lax.all_to_all(joint, ("y", "near"), 0, 0, tiled=True)
    gated, power = call(
        functools.partial(carry_kernel, heads, blocks),
        (((rows, width), f32), ((HEAD, rows // LANES, LANES), f32)),
        [VMEM] * 6,
        16 * MIB,
        1 << 28,
        8 * MIB,
    )(entering, own, lead, read_proj, base, factor)
    powers = lax.all_to_all(power, "head", 0, 0, tiled=True)
    (out,) = call(
        functools.partial(norm_kernel, heads),
        (((rows, width), bf16),),
        [VMEM] * 3,
        8 * MIB,
        1 << 20,
        3 * MIB,
        (pltpu.VMEM((rows, width), bf16), pltpu.SemaphoreType.DMA((rows // LANES,))),
        HBM,
    )(powers, norm_gain.reshape(1, width), gated)
    return out


def solution(mesh):
    split = Mesh(mesh.devices.reshape(Y, FAR, NEAR, HEAD), ("y", "far", "near", "head"))
    seq = ("y", "far", "near")
    placed = (
        P(seq, "head"),
        P(seq, "head"),
        P(seq, None),
        P(seq, None),
        P("head", seq),
        P("head"),
        P("head"),
        P("head"),
    )
    return jax.shard_map(local, mesh=split, in_specs=placed, out_specs=P(seq, "head"), check_vma=False)
```

```python
import functools
import math

import jax
import jax.numpy as jnp
from jax import lax
from jax.experimental import pallas as pl
from jax.experimental.pallas import tpu as pltpu
from jax.sharding import Mesh
from jax.sharding import PartitionSpec as P

GROUP = 256
HALF = 128
LANES = 128
CODE_SCALE = 524288.0
CHANNELS = 4096
EPS = 1e-05
Y, FAR, NEAR, HEAD = 4, 4, 4, 8
STATE = 128
OWNERS = Y * NEAR
PIECE = 32
PIECE_ROWS = 33
TOTAL_ROWS = Y * PIECE + 8
MIB = 1 << 20
NT = (((1,), (1,)), ((), ()))
TN = (((0,), (0,)), ((), ()))


def matmul(a, b, dims=(((1,), (0,)), ((), ()))):
    return lax.dot_general(a, b, dims, preferred_element_type=jnp.float32)


def lower_triangle(size):
    row = lax.broadcasted_iota(jnp.int32, (size, size), 0)
    column = lax.broadcasted_iota(jnp.int32, (size, size), 1)
    return row >= column


def code_parts(codes, heads, blocks):
    rows = jnp.concatenate([codes[:, k * GROUP : (k + 1) * GROUP] for k in range(blocks)], axis=0)
    parts = [rows & 255, (rows >> 8) & 255, rows >> 16]
    return jnp.concatenate([part.astype(jnp.float32) for part in parts], axis=0).astype(jnp.bfloat16)


def joined(sums, axis):
    count = sums.shape[axis] // 3
    low, middle, high = (lax.slice_in_dim(sums, i * count, (i + 1) * count, axis=axis) for i in range(3))
    return low + 256.0 * middle + 65536.0 * high


def code_columns(parts, triangle):
    return joined(matmul(triangle, parts, NT), 1)


def code_rows(parts, triangle):
    return joined(matmul(parts, triangle, NT), 0)


def exponent_row(rate_ref, heads, blocks):
    lane = lax.broadcasted_iota(jnp.int32, (1, blocks * heads), 1)
    row = jnp.zeros((1, blocks * heads), jnp.float32)
    for h in range(heads):
        row = jnp.where(lax.rem(lane, heads) == h, rate_ref[h], row)
    return row * (-1.0 / (CODE_SCALE * math.log(2.0)))


def head_lanes(row, start, heads):
    return jnp.concatenate(
        [jnp.broadcast_to(row[:, start + h : start + h + 1], (1, LANES)) for h in range(heads)], axis=1
    )


def weighted_inputs(tail, x_ref, rows, k, heads):
    return jnp.concatenate(
        [
            (tail[:, k * heads + h : k * heads + h + 1] * x_ref[rows, h * LANES : (h + 1) * LANES].astype(jnp.float32))
            .astype(jnp.bfloat16)
            for h in range(heads)
        ],
        axis=1,
    )


def summary_kernel(
    heads,
    blocks,
    rate_hbm,
    codes_hbm,
    write_hbm,
    x_hbm,
    piece_ref,
    rate_ref,
    codes_ref,
    write_ref,
    x_ref,
    sem,
):
    pairs = ((rate_hbm, rate_ref), (codes_hbm, codes_ref), (write_hbm, write_ref), (x_hbm, x_ref))
    copies = [pltpu.make_async_copy(a, b, sem.at[i]) for i, (a, b) in enumerate(pairs)]
    for copy in copies:
        copy.start()
    triangle = lower_triangle(GROUP).astype(jnp.float32).astype(jnp.bfloat16)
    for copy in copies[:2]:
        copy.wait()
    sums = code_columns(code_parts(codes_ref[...], heads, blocks), triangle)
    scale = exponent_row(rate_ref, heads, blocks)
    ends = sums[GROUP - 1 : GROUP, :]
    tail = jnp.exp2((ends - sums) * scale)
    block_decay = jnp.exp2(ends * scale)
    total = sum(ends[:, k * heads : (k + 1) * heads] for k in range(blocks))
    section_decay = jnp.exp2(total * scale[:, :heads])
    for copy in copies[2:]:
        copy.wait()
    state = None
    for k in range(blocks):
        rows = pl.ds(k * GROUP, GROUP)
        added = matmul(write_ref[rows, :], weighted_inputs(tail, x_ref, rows, k, heads), TN)
        state = head_lanes(block_decay, k * heads, heads) * state + added if k else added
    quarters = STATE // PIECE
    for h in range(heads):
        decay = jnp.broadcast_to(section_decay[:, h : h + 1], (PIECE_ROWS - PIECE, LANES))
        for q in range(quarters):
            piece_ref[h * quarters + q, :PIECE, :] = state[q * PIECE : (q + 1) * PIECE, h * LANES : (h + 1) * LANES]
            piece_ref[h * quarters + q, PIECE:, :] = decay


def inner_kernel(
    heads,
    blocks,
    rate_hbm,
    skip_hbm,
    codes_hbm,
    write_hbm,
    read_hbm,
    x_hbm,
    gate_hbm,
    base_ref,
    factor_ref,
    lead_ref,
    local_ref,
    rate_ref,
    skip_ref,
    codes_ref,
    write_ref,
    read_ref,
    x_ref,
    gate_ref,
    sem,
):
    sources = (rate_hbm, skip_hbm, codes_hbm, write_hbm, read_hbm, x_hbm, gate_hbm)
    targets = (rate_ref, skip_ref, codes_ref, write_ref, read_ref, x_ref, gate_ref)
    copies = [pltpu.make_async_copy(a, b, sem.at[i]) for i, (a, b) in enumerate(zip(sources, targets, strict=True))]
    for copy in copies:
        copy.start()
    for copy in copies:
        copy.wait()
    causal = lower_triangle(GROUP)
    triangle = causal.astype(jnp.float32).astype(jnp.bfloat16)
    corner = lower_triangle(HALF)
    parts = code_parts(codes_ref[...], heads, blocks)
    columns = code_columns(parts, triangle)
    across = code_rows(parts, triangle)
    scale = exponent_row(rate_ref, heads, blocks)
    grown = jnp.exp2(columns * scale)
    ends = columns[GROUP - 1 : GROUP, :]
    tail = jnp.exp2((ends - columns) * scale)
    block_decay = jnp.exp2(ends * scale)
    state = None
    for k in range(blocks - 1):
        rows = pl.ds(k * GROUP, GROUP)
        added = matmul(write_ref[rows, :], weighted_inputs(tail, x_ref, rows, k, heads), TN)
        state = head_lanes(block_decay, k * heads, heads) * state + added if k else added
        local_ref[k] = state
    before = jnp.zeros((1, heads), jnp.float32)
    for k in range(blocks):
        lead_ref[k : k + 1, :] = head_lanes(jnp.exp2(before * scale[:, :heads]), 0, heads)
        before = before + ends[:, k * heads : (k + 1) * heads]
    for k in range(blocks):
        rows = pl.ds(k * GROUP, GROUP)
        scores = matmul(read_ref[rows, :], write_ref[rows, :], NT)
        for h in range(heads):
            at = k * heads + h
            lanes = slice(h * LANES, (h + 1) * LANES)
            factor = scale[:, h : h + 1]
            column = columns[:, at : at + 1]
            row = across[at : at + 1, :]

            def mixed(t0, t1, s0, s1, masked):
                decay = jnp.exp2((column[t0:t1] - row[:, s0:s1]) * factor) * scores[t0:t1, s0:s1]
                if masked:
                    decay = jnp.where(corner, decay, 0.0)
                return decay.astype(jnp.bfloat16)

            x_part = x_ref[rows, lanes]
            upper = matmul(mixed(0, HALF, 0, HALF, True), x_part[:HALF])
            lower = jnp.concatenate(
                [mixed(HALF, GROUP, 0, HALF, False), mixed(HALF, GROUP, HALF, GROUP, True)], axis=1
            )
            inner = jnp.concatenate([upper, matmul(lower, x_part)], axis=0)
            gate = gate_ref[rows, lanes].astype(jnp.float32)
            silu = gate / (1.0 + jnp.exp(-gate))
            base_ref[rows, lanes] = (inner + skip_ref[h] * x_part.astype(jnp.float32)) * silu
            factor_ref[rows, lanes] = grown[:, at : at + 1] * silu


def near_kernel(got_ref, prefix_ref, decay_ref, total_ref):
    place = lax.broadcasted_iota(jnp.int32, (TOTAL_ROWS - Y * PIECE, LANES), 0)
    decays = jnp.zeros((TOTAL_ROWS - Y * PIECE, LANES), jnp.float32)
    totals = []
    for y in range(Y):
        state = jnp.zeros((PIECE, LANES), jnp.float32)
        decay = jnp.ones((PIECE_ROWS - PIECE, LANES), jnp.float32)
        for i in range(y * NEAR, (y + 1) * NEAR):
            prefix_ref[i] = state
            decay_ref[i] = decay
            step = got_ref[i, PIECE:, :]
            state = step[:1] * state + got_ref[i, :PIECE, :]
            decay = step * decay
        totals.append(state)
        decays = jnp.where(place == y, decay, decays)
    for y in range(Y):
        total_ref[y * PIECE : (y + 1) * PIECE, :] = totals[y]
    total_ref[Y * PIECE :, :] = decays


def join_kernel(got_ref, prefix_ref, decay_ref, out_ref):
    mine = lax.axis_index("far")
    state = jnp.zeros((PIECE, LANES), jnp.float32)
    for y in range(Y):
        own = state
        for i in range(FAR):
            own = jnp.where(i == mine, state, own)
            decay = got_ref[i, Y * PIECE + y : Y * PIECE + y + 1, :]
            state = decay * state + got_ref[i, y * PIECE : (y + 1) * PIECE, :]
        for i in range(y * NEAR, (y + 1) * NEAR):
            out_ref[i] = decay_ref[i, :1, :] * own + prefix_ref[i]


def carry_kernel(heads, blocks, entering_ref, local_ref, lead_ref, read_ref, base_ref, factor_ref, gated_ref, power_ref):
    quarters = STATE // PIECE
    entering = jnp.concatenate(
        [
            jnp.concatenate([entering_ref[h * quarters + q] for q in range(quarters)], axis=0)
            for h in range(heads)
        ],
        axis=1,
    )
    sums = []
    for k in range(blocks):
        rows = pl.ds(k * GROUP, GROUP)
        state = lead_ref[k : k + 1, :] * entering + local_ref[k - 1] if k else entering
        read_out = matmul(read_ref[rows, :], state.astype(jnp.bfloat16))
        gated = base_ref[rows, :] + factor_ref[rows, :] * read_out
        gated_ref[rows, :] = gated
        squares = gated * gated
        squares = sum(squares[:, h * LANES : (h + 1) * LANES] for h in range(heads))
        for half in range(GROUP // LANES):
            sums.append(jnp.sum(squares[half * LANES : (half + 1) * LANES].T, axis=0, keepdims=True))
    sums = jnp.concatenate(sums, axis=0)
    for j in range(HEAD):
        power_ref[j] = sums


def norm_kernel(heads, power_ref, gain_ref, gated_ref, out_hbm, out_ref, out_sem):
    power = sum(power_ref[j] for j in range(HEAD)) * (1.0 / CHANNELS)
    scale = lax.rsqrt(power + EPS)
    copies = []
    for r in range(scale.shape[0]):
        rows = pl.ds(r * LANES, LANES)
        column = jnp.broadcast_to(scale[r : r + 1, :], (LANES, LANES)).T
        for h in range(heads):
            lanes = slice(h * LANES, (h + 1) * LANES)
            out_ref[rows, lanes] = (gated_ref[rows, lanes] * column * gain_ref[:, lanes]).astype(jnp.bfloat16)
        copies.append(pltpu.make_async_copy(out_ref.at[rows], out_hbm.at[rows], out_sem.at[r]))
        copies[-1].start()
    for copy in copies:
        copy.wait()


VMEM = pl.BlockSpec(memory_space=pltpu.VMEM)
SMEM = pl.BlockSpec(memory_space=pltpu.SMEM)
HBM = pl.BlockSpec(memory_space=pltpu.HBM)


def call(kernel, out_shapes, in_specs, limit, flops, moved, scratch=(), out_spec=VMEM):
    return pl.pallas_call(
        kernel,
        out_shape=tuple(jax.ShapeDtypeStruct(shape, dtype) for shape, dtype in out_shapes),
        in_specs=in_specs,
        out_specs=tuple(out_spec for _ in out_shapes),
        scratch_shapes=scratch,
        compiler_params=pltpu.CompilerParams(vmem_limit_bytes=limit),
        cost_estimate=pl.CostEstimate(flops=flops, bytes_accessed=moved, transcendentals=0),
    )


def in_hbm(*arrays):
    return tuple(pltpu.with_memory_space_constraint(array, pltpu.HBM) for array in arrays)


def local(ssm_input, gate_input, write_proj, read_proj, decay_codes, decay_rate, skip_gain, norm_gain):
    rows, width = ssm_input.shape
    heads = decay_rate.shape[0]
    blocks = rows // GROUP
    f32, bf16 = jnp.float32, jnp.bfloat16
    (piece,) = call(
        functools.partial(summary_kernel, heads, blocks),
        (((OWNERS, PIECE_ROWS, LANES), f32),),
        [HBM] * 4,
        8 * MIB,
        1 << 28,
        3 * MIB,
        (
            pltpu.SMEM(decay_rate.shape, f32),
            pltpu.VMEM(decay_codes.shape, jnp.int32),
            pltpu.VMEM(write_proj.shape, bf16),
            pltpu.VMEM(ssm_input.shape, bf16),
            pltpu.SemaphoreType.DMA((4,)),
        ),
    )(*in_hbm(decay_rate, decay_codes, write_proj, ssm_input))
    got = lax.all_to_all(piece, ("y", "near"), 0, 0, tiled=True)
    base, factor, lead, own = call(
        functools.partial(inner_kernel, heads, blocks),
        (((rows, width), f32), ((rows, width), f32), ((blocks, width), f32), ((blocks - 1, STATE, width), f32)),
        [HBM] * 7,
        16 * MIB,
        1 << 30,
        7 * MIB,
        (
            pltpu.SMEM(decay_rate.shape, f32),
            pltpu.SMEM(skip_gain.shape, f32),
            pltpu.VMEM(decay_codes.shape, jnp.int32),
            pltpu.VMEM(write_proj.shape, bf16),
            pltpu.VMEM(read_proj.shape, bf16),
            pltpu.VMEM(ssm_input.shape, bf16),
            pltpu.VMEM(gate_input.shape, bf16),
            pltpu.SemaphoreType.DMA((7,)),
        ),
    )(*in_hbm(decay_rate, skip_gain, decay_codes, write_proj, read_proj, ssm_input, gate_input))
    got, base, factor, lead, own = lax.optimization_barrier((got, base, factor, lead, own))
    prefix, prefix_decay, total = call(
        near_kernel,
        (((OWNERS, PIECE, LANES), f32), ((OWNERS, PIECE_ROWS - PIECE, LANES), f32), ((TOTAL_ROWS, LANES), f32)),
        [VMEM],
        8 * MIB,
        1 << 33,
        MIB,
    )(got)
    totals = lax.all_gather(total, "far")
    (joint,) = call(join_kernel, (((OWNERS, PIECE, LANES), f32),), [VMEM] * 3, 8 * MIB, 1 << 33, MIB)(
        totals, prefix, prefix_decay
    )
    entering = lax.all_to_all(joint, ("y", "near"), 0, 0, tiled=True)
    gated, power = call(
        functools.partial(carry_kernel, heads, blocks),
        (((rows, width), f32), ((HEAD, rows // LANES, LANES), f32)),
        [VMEM] * 6,
        16 * MIB,
        1 << 28,
        8 * MIB,
    )(entering, own, lead, read_proj, base, factor)
    powers = lax.all_to_all(power, "head", 0, 0, tiled=True)
    (out,) = call(
        functools.partial(norm_kernel, heads),
        (((rows, width), bf16),),
        [VMEM] * 3,
        8 * MIB,
        1 << 20,
        3 * MIB,
        (pltpu.VMEM((rows, width), bf16), pltpu.SemaphoreType.DMA((rows // LANES,))),
        HBM,
    )(powers, norm_gain.reshape(1, width), gated)
    return out


def solution(mesh):
    split = Mesh(mesh.devices.reshape(Y, FAR, NEAR, HEAD), ("y", "far", "near", "head"))
    seq = ("y", "far", "near")
    placed = (
        P(seq, "head"),
        P(seq, "head"),
        P(seq, None),
        P(seq, None),
        P("head", seq),
        P("head"),
        P("head"),
        P("head"),
    )
    return jax.shard_map(local, mesh=split, in_specs=placed, out_specs=P(seq, "head"), check_vma=False)
```
